128 devices in a mesh: dp: 16 (over y_lo, x, core), tensor: 8 (over y_hi, z).
Axes of the slice: x: 4, y: 4 (y_hi: 2, y_lo: 2; y = y_hi * 2 + y_lo), z: 4, core: 2. Of those that a mesh axis runs over, the one named last changes fastest.
Arguments:
- block_input: bfloat16 [16, 1024, 1024], P('dp', 'tensor'), may hold values from -6 to 6
- mixer_gain: float32 [1, 1024], replicated, may hold values from 0.25 to 1.75
- query_key_weight: bfloat16 [1, 1024, 8, 256], P(None, 'dp', 'tensor'), may hold values from -0.1875 to 0.1875
- value_gate_weight: bfloat16 [1, 1024, 8, 512], P(None, 'dp', 'tensor'), may hold values from -0.1875 to 0.1875
- beta_decay_weight: bfloat16 [1, 1024, 8, 2], P(None, 'dp', 'tensor'), may hold values from -0.1875 to 0.1875
- conv_query_key: float32 [1, 4, 8, 256], P(None, None, 'tensor'), may hold values from -3 to 3
- conv_value: float32 [1, 4, 8, 256], P(None, None, 'tensor'), may hold values from -3 to 3
- decay_log: float32 [1, 8], P(None, 'tensor'), may hold values from 0 to 0.7
- decay_bias: float32 [1, 8], P(None, 'tensor'), may hold values from -6.9 to -4.2
- out_gain: float32 [1, 256], replicated, may hold values from 0.25 to 1.75
- out_weight: bfloat16 [1, 8, 256, 1024], P(None, 'tensor', None, 'dp'), may hold values from -0.25 to 0.25
- forward_gain: float32 [1, 1024], replicated, may hold values from 0.25 to 1.75
- gate_up_weight: bfloat16 [1, 1024, 2, 2816], P(None, 'dp', None, 'tensor'), may hold values from -0.1875 to 0.1875
- down_weight: bfloat16 [1, 2816, 1024], P(None, 'tensor', 'dp'), may hold values from -0.21875 to 0.21875
- out_cotangent: bfloat16 [16, 1024, 1024], P('dp', 'tensor'), may hold values from -6 to 6
Outputs:
- block_output: float32 [16, 1024, 1024], P('dp', 'tensor')
- input_grad: float32 [16, 1024, 1024], P('dp', 'tensor')
- grad_mixer_gain: float32 [1, 1024], replicated
- grad_query_key: float32 [1, 1024, 8, 256], P(None, 'dp', 'tensor')
- grad_value_gate: float32 [1, 1024, 8, 512], P(None, 'dp', 'tensor')
- grad_beta_decay: float32 [1, 1024, 8, 2], P(None, 'dp', 'tensor')
- grad_conv_query_key: float32 [1, 4, 8, 256], P(None, None, 'tensor')
- grad_conv_value: float32 [1, 4, 8, 256], P(None, None, 'tensor')
- grad_decay_log: float32 [1, 8], P(None, 'tensor')
- grad_decay_bias: float32 [1, 8], P(None, 'tensor')
- grad_out_gain: float32 [1, 256], replicated
- grad_out_weight: float32 [1, 8, 256, 1024], P(None, 'tensor', None, 'dp')
- grad_forward_gain: float32 [1, 1024], replicated
- gradient_gate_up_weight: float32 [1, 1024, 2, 2816], P(None, 'dp', None, 'tensor')
- grad_down: float32 [1, 2816, 1024], P(None, 'tensor', 'dp')
The draws below stay inside these ranges and needn't reach their ends.
All inputs are finite; a program needn't handle non-finite values.
Results may differ from the reference program's by a relative error of at most 0.02.
Values may be sent and summed in bfloat16 or wider, within the bound.
A program may use at most 128 MiB of HBM per device.

```python
import jax
import jax.numpy as jnp
from jax import lax

D = 1024
H = 8
DK = 128
DV = 256
FF = 2816
CONV = 4
SPAN = 64
LAYERS = 1
LENGTH = 1024
BATCH = 16


def block_scale(key, shape, shards, smallest, high):
    def one(dim, shards_of):
        steps = jax.random.uniform(jax.random.fold_in(jax.random.fold_in(key, 6), dim), (shards_of,), jnp.float32, smallest / len(shards), high / len(shards))
        return jnp.repeat(jnp.exp(steps), shape[dim] // shards_of).reshape((-1,) + (1,) * (len(shape) - dim - 1))

    level = one(*shards[0])
    for cut in shards[1:]:
        level = level * one(*cut)
    return level


def normal_values(own_key, extent, width, bound, split=(), held_as=jnp.bfloat16):
    factor_of = block_scale(own_key, extent, split, -0.22, 0.18) if split else 1.0
    entries = jax.random.normal(own_key, extent, jnp.float32) * width * factor_of
    return jnp.minimum(jnp.maximum(entries, -bound), bound).astype(held_as)


def setup_inputs(seed: int = 0) -> dict:
    key_of = jax.random.split(jax.random.key(seed), 16)
    block_input = normal_values(key_of[0], (BATCH, LENGTH, D), 1.0, 6.0, ((0, 16), (1, 8)))
    mixer_gain = jnp.clip(1.0 + 0.15 * jax.random.normal(key_of[1], (LAYERS, D), jnp.float32), 0.25, 1.75)
    query_key_weight = normal_values(key_of[2], (LAYERS, D, H, 2 * DK), D ** -0.5, 0.1875, ((1, 16), (2, 8)))
    value_gate_weight = normal_values(key_of[3], (LAYERS, D, H, 2 * DV), D ** -0.5, 0.1875, ((1, 16), (2, 8)))
    beta_decay_weight = normal_values(key_of[4], (LAYERS, D, H, 2), D ** -0.5, 0.1875, ((1, 16), (2, 8)))
    conv_query_key = normal_values(key_of[5], (LAYERS, CONV, H, 2 * DK), CONV ** -0.5, 3.0, ((2, 8),), jnp.float32)
    conv_value = normal_values(key_of[6], (LAYERS, CONV, H, DV), CONV ** -0.5, 3.0, ((2, 8),), jnp.float32)
    decay_log = jnp.clip(0.7 * jax.random.uniform(key_of[7], (LAYERS, H), jnp.float32) ** block_scale(key_of[7], (LAYERS, H), ((1, 8),), -0.2, 0.2), 0.0, 0.7)
    decay_bias = jnp.clip(-6.9 + 2.7000003 * jax.random.uniform(key_of[8], (LAYERS, H), jnp.float32) ** block_scale(key_of[8], (LAYERS, H), ((1, 8),), -0.2, 0.2), -6.9, -4.2)
    out_gain = jnp.clip(1.0 + 0.15 * jax.random.normal(key_of[9], (LAYERS, DV), jnp.float32), 0.25, 1.75)
    out_weight = normal_values(key_of[10], (LAYERS, H, DV, D), (H * DV // 4) ** -0.5, 0.25, ((1, 8), (3, 16)))
    forward_gain = jnp.clip(1.0 + 0.15 * jax.random.normal(key_of[11], (LAYERS, D), jnp.float32), 0.25, 1.75)
    gate_up_weight = normal_values(key_of[12], (LAYERS, D, 2, FF), D ** -0.5, 0.1875, ((1, 16), (3, 8)))
    down_weight = normal_values(key_of[13], (LAYERS, FF, D), (FF // 4) ** -0.5, 0.21875, ((1, 8), (2, 16)))
    out_cotangent = normal_values(key_of[14], (BATCH, LENGTH, D), 1.0, 6.0, ((0, 16), (1, 8)))
    return {"block_input": block_input, "mixer_gain": mixer_gain, "query_key_weight": query_key_weight, "value_gate_weight": value_gate_weight, "beta_decay_weight": beta_decay_weight, "conv_query_key": conv_query_key, "conv_value": conv_value, "decay_log": decay_log, "decay_bias": decay_bias, "out_gain": out_gain, "out_weight": out_weight, "forward_gain": forward_gain, "gate_up_weight": gate_up_weight, "down_weight": down_weight, "out_cotangent": out_cotangent}


@jax.custom_vjp
def low(v):
    return lax.optimization_barrier(v.astype(jnp.bfloat16)).astype(jnp.float32)

@jax.custom_vjp
def low_back(v):
    return v

def low_keep(v):
    return (low(v), None)

def low_pass(kept, grad):
    return (grad,)

def back_keep(v):
    return (v, None)

def back_low(kept, grad):
    return (low(grad),)
low.defvjp(low_keep, low_pass)
low_back.defvjp(back_keep, back_low)
EPS = 1e-06
GATED_EPS = 1e-05
PRECISE = lax.Precision.HIGHEST

def norm_rows(values, gain, offset=EPS):
    return values * lax.rsqrt(lax.optimization_barrier(jnp.mean(values * values, -1, keepdims=True)) + offset) * gain

def causal_conv(inputs, taps):
    length = inputs.shape[0]
    padded = jnp.pad(inputs, ((taps.shape[0] - 1, 0), (0, 0), (0, 0)))
    summed = padded[0:length] * taps[0]
    for shift_at in range(1, taps.shape[0]):
        summed = summed + padded[shift_at:shift_at + length] * taps[shift_at]
    return summed

def span_step(memory, block):
    queries, keys_in, values_in, beta_rows, log_decay = block
    block_len = log_decay.shape[0]
    cumulative = jnp.cumsum(log_decay)
    row_index = lax.broadcasted_iota(jnp.int32, (block_len, block_len), 0)
    col_index = lax.broadcasted_iota(jnp.int32, (block_len, block_len), 1)
    lower_eq = (row_index >= col_index).astype(jnp.float32)
    strict_lower = (row_index > col_index).astype(jnp.float32)
    decay_table = jnp.exp(jnp.where(row_index >= col_index, cumulative[:, None] - cumulative[None, :], 0.0)) * lower_eq
    scale_in = jnp.exp(cumulative)
    key_inner = jnp.dot(keys_in, keys_in.T, precision=PRECISE)
    system = jnp.eye(block_len, dtype=jnp.float32) + beta_rows[:, None] * key_inner * decay_table * strict_lower
    right_side = beta_rows[:, None] * (values_in - scale_in[:, None] * jnp.dot(keys_in, memory, precision=PRECISE))
    updates = jax.scipy.linalg.solve_triangular(system, right_side, lower=True, unit_diagonal=True)
    scores = jnp.dot(queries, keys_in.T, precision=PRECISE) * decay_table
    output = scale_in[:, None] * jnp.dot(queries, memory, precision=PRECISE) + jnp.dot(scores, updates, precision=PRECISE)
    tail_decay = jnp.exp(cumulative[-1] - cumulative)
    new_memory = jnp.exp(cumulative[-1]) * memory + jnp.dot((keys_in * tail_decay[:, None]).T, updates, precision=PRECISE)
    return (new_memory, output)

def delta_head(queries, keys_in, values_in, beta_rows, log_decay):
    length = queries.shape[0]
    blocks = (queries.reshape(-1, SPAN, queries.shape[-1]), keys_in.reshape(-1, SPAN, keys_in.shape[-1]), values_in.reshape(-1, SPAN, values_in.shape[-1]), beta_rows.reshape(-1, SPAN), log_decay.reshape(-1, SPAN))
    start = jnp.zeros((queries.shape[-1], values_in.shape[-1]), jnp.float32)
    final_memory, outputs = lax.scan(jax.checkpoint(span_step), start, blocks)
    return outputs.reshape(length, values_in.shape[-1])

def mixer_core(query_key_pre, value_gate_pre, beta_decay_pre, conv_query_key, conv_value, decay_log, decay_bias, out_gain):
    head_dim = query_key_pre.shape[-1] // 2
    value_dim = value_gate_pre.shape[-1] // 2
    conv_rows = jax.nn.silu(causal_conv(query_key_pre, conv_query_key))
    queries = conv_rows[..., :head_dim]
    keys_in = conv_rows[..., head_dim:]
    queries = queries * lax.rsqrt(lax.optimization_barrier(jnp.sum(queries * queries, -1, keepdims=True)) + EPS) * head_dim ** (-0.5)
    keys_in = keys_in * lax.rsqrt(lax.optimization_barrier(jnp.sum(keys_in * keys_in, -1, keepdims=True)) + EPS)
    values_in = jax.nn.silu(causal_conv(value_gate_pre[..., :value_dim], conv_value))
    gates = value_gate_pre[..., value_dim:]
    beta_rows = jax.nn.sigmoid(beta_decay_pre[..., 0])
    log_decay = -jnp.exp(decay_log) * jax.nn.softplus(beta_decay_pre[..., 1] + decay_bias)
    delta_out = jax.vmap(delta_head, in_axes=1, out_axes=1)(queries, keys_in, values_in, beta_rows, log_decay)
    return norm_rows(delta_out, out_gain, GATED_EPS) * jax.nn.silu(gates)

def layer_pair(sequence, params):
    mixer_gain, query_key_weight, value_gate_weight, beta_decay_weight, conv_query_key, conv_value, decay_log, decay_bias, out_gain, out_weight, forward_gain, gate_up_weight, down_weight = params
    length = sequence.shape[0]
    for layer_num in range(LAYERS):
        normed = low(norm_rows(sequence, mixer_gain[layer_num]))
        query_key_pre = low_back(jnp.einsum('ld,dhc->lhc', normed, query_key_weight[layer_num], precision=PRECISE))
        value_gate_pre = low_back(jnp.einsum('ld,dhc->lhc', normed, value_gate_weight[layer_num], precision=PRECISE))
        beta_decay_pre = low_back(jnp.einsum('ld,dhc->lhc', normed, beta_decay_weight[layer_num], precision=PRECISE))
        mixed = low(mixer_core(query_key_pre, value_gate_pre, beta_decay_pre, conv_query_key[layer_num], conv_value[layer_num], decay_log[layer_num], decay_bias[layer_num], out_gain[layer_num]))
        mixer_branch = jnp.einsum('lhc,hcd->ld', mixed, out_weight[layer_num], precision=PRECISE)
        sequence = sequence + low_back(mixer_branch)
        normed = low(norm_rows(sequence, forward_gain[layer_num]))
        gate_up = low_back(jnp.einsum('ld,dkf->lkf', normed, gate_up_weight[layer_num], precision=PRECISE))
        hidden_activation = low(jax.nn.silu(gate_up[:, 0]) * gate_up[:, 1])
        forward_branch = jnp.dot(hidden_activation, down_weight[layer_num], precision=PRECISE)
        sequence = sequence + low_back(forward_branch)
    return sequence

def reference(block_input, mixer_gain, query_key_weight, value_gate_weight, beta_decay_weight, conv_query_key, conv_value, decay_log, decay_bias, out_gain, out_weight, forward_gain, gate_up_weight, down_weight, out_cotangent):
    params = tuple((item.astype(jnp.float32) for item in (mixer_gain, query_key_weight, value_gate_weight, beta_decay_weight, conv_query_key, conv_value, decay_log, decay_bias, out_gain, out_weight, forward_gain, gate_up_weight, down_weight)))

    def forward(stream, *weights):

        def one_sequence(sequence):
            return layer_pair(sequence, weights)
        return lax.map(jax.checkpoint(one_sequence), stream)
    block_output, backward = jax.vjp(forward, block_input.astype(jnp.float32), *params)
    grads = backward(out_cotangent.astype(jnp.float32))
    return (block_output, grads[0], grads[1], grads[2], grads[3], grads[4], grads[5], grads[6], grads[7], grads[8], grads[9], grads[10], grads[11], grads[12], grads[13])
```

```python
import functools

import jax
import jax.numpy as jnp
from jax import lax
from jax.experimental import pallas as pl
from jax.experimental.pallas import tpu as pltpu
from jax.sharding import PartitionSpec as P
C = 128
HI = lax.Precision.HIGHEST
LO = lax.Precision.DEFAULT
F32 = jnp.float32
NN = (((1,), (0,)), ((), ()))
NT = (((1,), (1,)), ((), ()))
TN = (((0,), (0,)), ((), ()))


def mm(a, b, dims=NN, precision=HI):
    return lax.dot_general(a, b, dims, precision=precision, preferred_element_type=F32)


def chunk_masks():
    row = lax.broadcasted_iota(jnp.int32, (C, C), 0)
    col = lax.broadcasted_iota(jnp.int32, (C, C), 1)
    return row, col


def decay_parts(g, row, col):
    lower = (row >= col).astype(F32)
    cum = mm(lower, g)
    table = jnp.where(row >= col, jnp.exp(jnp.where(row >= col, cum - cum.T, 0.0)), 0.0)
    last = cum[C - 1 : C, :]
    return table, jnp.exp(cum), jnp.exp(last - cum), jnp.exp(last)


def wide(x):
    return jnp.concatenate([x, x], axis=1)


def inverse_many(systems, row, col, prec):
    eye = (row == col).astype(F32)
    near = (row // 8) == (col // 8)
    a1 = [jnp.where(near, a, 0.0) for a in systems]
    a2 = [mm(a, a, precision=prec) for a in a1]
    x = [eye - a for a in a1]
    a4 = [mm(a, a, precision=prec) for a in a2]
    x = [y + mm(y, a, precision=prec) for y, a in zip(x, a2)]
    x = [y + mm(y, a, precision=prec) for y, a in zip(x, a4)]
    size = 8
    while size < C:
        pick = ((row // (2 * size)) == (col // (2 * size))) & ((row // size) != (col // size))
        off = [jnp.where(pick, a, 0.0) for a in systems]
        y = [mm(o, t, precision=prec) for o, t in zip(off, x)]
        x = [t - mm(t, z, precision=prec) for t, z in zip(x, y)]
        size *= 2
    return x


def fwd_kernel(P_, group, q_ref, k_ref, v_ref, b_ref, g_ref, o_ref, t_ref, u_ref, s_ref, f_ref, w_ref, z_ref):
    nb = q_ref.shape[0] // C
    row, col = chunk_masks()

    def first(i, _):
        cs = [pl.ds(pl.multiple_of((i * group + j) * C, C), C) for j in range(group)]
        q = [q_ref[c, :] for c in cs]
        k = [k_ref[c, :] for c in cs]
        v = [v_ref[c, :] for c in cs]
        b = [b_ref[c, :] for c in cs]
        parts = [decay_parts(g_ref[c, :], row, col) for c in cs]
        kk = [mm(x, x, NT, P_["kk"]) for x in k]
        system = [jnp.where(row > col, bb * x * p[0], 0.0) for bb, x, p in zip(b, kk, parts)]
        t = inverse_many(system, row, col, P_["inv"])
        w = [mm(tt, bb * p[1] * x, precision=P_["w"]) for tt, bb, p, x in zip(t, b, parts, k)]
        u0 = [mm(tt, wide(bb) * x, precision=P_["u"]) for tt, bb, x in zip(t, b, v)]
        kd = [x * p[2] for x, p in zip(k, parts)]
        eye = (row == col).astype(F32)
        for c, kdd, ww, uu, tt, p in zip(cs, kd, w, u0, t, parts):
            t_ref[c, :] = tt
            w_ref[c, :] = ww
            u_ref[c, :] = uu
            f_ref[c, :] = eye * p[3] - mm(kdd, ww, TN, P_["f"])
            z_ref[c, :] = mm(kdd, uu, TN, P_["z"])
        return 0

    lax.fori_loop(0, nb // group, first, 0)
    state = jnp.zeros((C, v_ref.shape[1]), F32)
    for i in range(nb):
        c = pl.ds(i * C, C)
        s_ref[c, :] = state
        if i < nb - 1:
            state = z_ref[c, :] + mm(f_ref[c, :], state, precision=P_["chain"])

    def last(i, _):
        cs = [pl.ds(pl.multiple_of((i * group + j) * C, C), C) for j in range(group)]
        for c in cs:
            q, k, s = q_ref[c, :], k_ref[c, :], s_ref[c, :]
            table, scale, _, _ = decay_parts(g_ref[c, :], row, col)
            u = u_ref[c, :] - mm(w_ref[c, :], s, precision=P_["ws"])
            u_ref[c, :] = u
            scores = mm(q, k, NT, P_["qk"]) * table
            o_ref[c, :] = mm(q * scale, s, precision=P_["o"]) + mm(scores, u, precision=P_["o"])
        return 0

    lax.fori_loop(0, nb // group, last, 0)


def bwd_kernel(P_, group, q_ref, k_ref, v_ref, b_ref, g_ref, t_ref, u_ref, s_ref, f_ref, w_ref, do_ref,
               dq_ref, dk_ref, dv_ref, db_ref, dg_ref, ds_ref, x_ref):
    nb = q_ref.shape[0] // C
    row, col = chunk_masks()

    def first(i, _):
        cs = [pl.ds(pl.multiple_of((i * group + j) * C, C), C) for j in range(group)]
        for c in cs:
            q, k, do = q_ref[c, :], k_ref[c, :], do_ref[c, :]
            table, scale, _, _ = decay_parts(g_ref[c, :], row, col)
            scores = mm(q, k, NT, P_["qk"]) * table
            x = mm(scores, do, TN, P_["bx"])
            x_ref[c, :] = x
            ds_ref[c, :] = mm(q * scale, do, TN, P_["bx"]) - mm(w_ref[c, :], x, TN, P_["bx"])
        return 0

    lax.fori_loop(0, nb // group, first, 0)
    carry = jnp.zeros((C, v_ref.shape[1]), F32)
    for i in reversed(range(nb)):
        c = pl.ds(i * C, C)
        own = ds_ref[c, :]
        ds_ref[c, :] = carry
        if i > 0:
            carry = own + mm(f_ref[c, :], carry, TN, P_["chain"])

    def last(i, _):
        cs = [pl.ds(pl.multiple_of((i * group + j) * C, C), C) for j in range(group)]
        for c in cs:
            q, k, v, b, do = q_ref[c, :], k_ref[c, :], v_ref[c, :], b_ref[c, :], do_ref[c, :]
            t, u, s, ds = t_ref[c, :], u_ref[c, :], s_ref[c, :], ds_ref[c, :]
            table, scale, tail, total = decay_parts(g_ref[c, :], row, col)
            p = P_["bl"]
            qk = mm(q, k, NT, p)
            kk = mm(k, k, NT, p)
            ks = mm(k, s, precision=p)
            qs = mm(q, s, precision=p)
            kd = k * tail
            du = x_ref[c, :] + mm(kd, ds, precision=p)
            dr = mm(t, du, TN, P_["bt"])
            dp = jnp.where(row >= col, mm(do, u, NT, p), 0.0)
            da = jnp.where(row > col, -mm(dr, u, NT, p), 0.0)
            dqk = dp * table
            dkk = da * b * table
            n = dqk * qk + dkk * kk
            dkd = mm(u, ds, NT, p)
            dq_ref[c, :] = scale * mm(do, s, NT, p) + mm(dqk, k, precision=p)
            bdr = wide(b) * dr
            dk_ref[c, :] = (
                mm(dqk, q, TN, p)
                + mm(dkk, k, precision=p)
                + mm(dkk, k, TN, p)
                + dkd * tail
                - scale * mm(bdr, s, NT, p)
            )
            dv_ref[c, :] = bdr
            sc2 = wide(scale)
            db = jnp.sum(dr * (v - sc2 * ks), 1, keepdims=True) + jnp.sum(da * table * kk, 1, keepdims=True)
            db_ref[c, :] = jnp.broadcast_to(db, (C, C))
            tails = jnp.sum(dkd * kd, 1, keepdims=True)
            dcum = (
                jnp.sum(n, 1, keepdims=True)
                - jnp.sum(n.T, 1, keepdims=True)
                + jnp.sum(sc2 * (do * qs - bdr * ks), 1, keepdims=True)
                - tails
            )
            dcum = jnp.broadcast_to(dcum, (C, C))
            extra = jnp.sum(tails) + jnp.sum(ds * s * wide(jnp.broadcast_to(total, (C, C))))
            upper = (row <= col).astype(F32)
            dg_ref[c, :] = mm(upper, dcum) + extra
        return 0

    lax.fori_loop(0, nb // group, last, 0)


KEYS = ("kk", "inv", "w", "u", "f", "z", "chain", "ws", "qk", "o", "bx", "bl", "bt")
PRECS = {key: HI for key in KEYS}
BF = jnp.bfloat16
EPS = 1e-06
GATED_EPS = 1e-05
DP, TP = "dp", "tensor"


def in_vmem(n):
    return [pl.BlockSpec(memory_space=pltpu.VMEM)] * n


def delta_fwd(q, k, v, b, g):
    n, dv = v.shape
    sh = lambda w: jax.ShapeDtypeStruct((n, w), F32)
    return pl.pallas_call(
        functools.partial(fwd_kernel, PRECS, 4),
        out_shape=[sh(dv), sh(C), sh(dv), sh(dv), sh(C), sh(C)],
        in_specs=in_vmem(5),
        out_specs=in_vmem(6),
        scratch_shapes=[pltpu.VMEM((n, dv), F32)],
        compiler_params=pltpu.CompilerParams(vmem_limit_bytes=48 * 2**20),
        name="delta_forward",
    )(q, k, v, b, g)


def delta_bwd(q, k, v, b, g, t, u, s, f, w, do):
    n, dv = v.shape
    sh = lambda w: jax.ShapeDtypeStruct((n, w), F32)
    return pl.pallas_call(
        functools.partial(bwd_kernel, PRECS, 2),
        out_shape=[sh(C), sh(C), sh(dv), sh(C), sh(C)],
        in_specs=in_vmem(11),
        out_specs=in_vmem(5),
        scratch_shapes=[pltpu.VMEM((n, dv), F32), pltpu.VMEM((n, dv), F32)],
        compiler_params=pltpu.CompilerParams(vmem_limit_bytes=48 * 2**20),
        name="delta_backward",
    )(q, k, v, b, g, t, u, s, f, w, do)


def spread_columns(x):
    return jnp.broadcast_to(x[:, None], (x.shape[0], C))


@jax.custom_vjp
def delta_rule(q, k, v, b, g):
    return delta_rule_fwd(q, k, v, b, g)[0]


def delta_rule_fwd(q, k, v, b, g):
    b, g = spread_columns(b), spread_columns(g)
    o, t, u, s, f, w = delta_fwd(q, k, v, b, g)
    return o, (q, k, v, b, g, t, u, s, f, w)


def delta_rule_bwd(kept, do):
    dq, dk, dv, db, dg = delta_bwd(*kept, do)
    return dq, dk, dv, db[:, 0], dg[:, 0]


delta_rule.defvjp(delta_rule_fwd, delta_rule_bwd)


def norm_rows(values, gain, offset=EPS):
    return values * lax.rsqrt(jnp.mean(values * values, -1, keepdims=True) + offset) * gain


def causal_conv(inputs, taps):
    length = inputs.shape[0]
    padded = jnp.pad(inputs, ((taps.shape[0] - 1, 0), (0, 0)))
    summed = padded[0:length] * taps[0]
    for shift_at in range(1, taps.shape[0]):
        summed = summed + padded[shift_at : shift_at + length] * taps[shift_at]
    return summed


def mixer_core(qk_pre, vg_pre, bd_pre, conv_qk, conv_v, decay_log, decay_bias, out_gain):
    dk, dv = qk_pre.shape[-1] // 2, vg_pre.shape[-1] // 2
    rows = jax.nn.silu(causal_conv(qk_pre, conv_qk))
    q, k = rows[:, :dk], rows[:, dk:]
    q = q * lax.rsqrt(jnp.sum(q * q, -1, keepdims=True) + EPS) * dk ** (-0.5)
    k = k * lax.rsqrt(jnp.sum(k * k, -1, keepdims=True) + EPS)
    v = jax.nn.silu(causal_conv(vg_pre[:, :dv], conv_v))
    b = jax.nn.sigmoid(bd_pre[:, 0])
    g = -jnp.exp(decay_log) * jax.nn.softplus(bd_pre[:, 1] + decay_bias)
    return norm_rows(delta_rule(q, k, v, b, g), out_gain, GATED_EPS) * jax.nn.silu(vg_pre[:, dv:])


def dot(a, b, dims=NN):
    return lax.dot_general(a, b, dims, preferred_element_type=F32)


def gather(x, axis):
    copies = jnp.broadcast_to(x, (lax.axis_size(axis), *x.shape))
    tiles = lax.all_to_all(copies, axis, split_axis=0, concat_axis=0, tiled=True)
    return tiles.reshape(-1, x.shape[1])


def scatter_sum(x, axis):
    n = lax.axis_size(axis)
    tiles = x.astype(BF).reshape(n, x.shape[0] // n, x.shape[1])
    tiles = lax.all_to_all(tiles, axis, 0, 0, tiled=True)
    return jnp.sum(tiles.astype(F32), axis=0)


def body(
    block_input,
    mixer_gain,
    query_key_weight,
    value_gate_weight,
    beta_decay_weight,
    conv_query_key,
    conv_value,
    decay_log,
    decay_bias,
    out_gain,
    out_weight,
    forward_gain,
    gate_up_weight,
    down_weight,
    out_cotangent,
):
    stream = block_input[0].astype(F32)
    nqk, nvg, nbd = query_key_weight.shape[-1], value_gate_weight.shape[-1], beta_decay_weight.shape[-1]
    ff = gate_up_weight.shape[-1]
    nout = out_weight.shape[2]
    first_pack = jnp.concatenate(
        [query_key_weight[0, :, 0], value_gate_weight[0, :, 0], beta_decay_weight[0, :, 0]], 1
    )
    second_pack = jnp.concatenate(
        [out_weight[0, 0].T, gate_up_weight[0].reshape(-1, 2 * ff), down_weight[0].T], 1
    )
    w_in = gather(first_pack, DP)
    rows = gather(norm_rows(stream, mixer_gain[0]).astype(BF), TP)
    g_rows = gather(out_cotangent[0], TP)
    w_rest = gather(second_pack, DP)
    w_out, w_gu, w_down = w_rest[:, :nout], w_rest[:, nout : nout + 2 * ff], w_rest[:, nout + 2 * ff :]
    w_qk, w_vg, w_bd = w_in[:, :nqk], w_in[:, nqk : nqk + nvg], w_in[:, nqk + nvg :]

    mixed, core_back = jax.vjp(
        mixer_core,
        dot(rows, w_qk),
        dot(rows, w_vg),
        dot(rows, w_bd),
        conv_query_key[0, :, 0],
        conv_value[0, :, 0],
        decay_log[0, 0],
        decay_bias[0, 0],
        out_gain[0],
    )
    mixed = mixed.astype(BF)
    before_forward = stream + scatter_sum(dot(mixed, w_out, NT), TP)
    forward_rows = gather(norm_rows(before_forward, forward_gain[0]).astype(BF), TP)
    gate = dot(forward_rows, w_gu[:, :ff])
    up = dot(forward_rows, w_gu[:, ff:])
    s = jax.nn.sigmoid(gate)
    hidden = (gate * s * up).astype(BF)
    grad_hidden = dot(g_rows, w_down)
    grad_gu = jnp.concatenate(
        [(grad_hidden * up * s * (1.0 + gate * (1.0 - s))).astype(BF), (grad_hidden * gate * s).astype(BF)], 1
    )
    grad_normed = scatter_sum(dot(grad_gu, w_gu, NT), TP)
    _, norm_back = jax.vjp(norm_rows, before_forward, forward_gain[0])
    grad_before, grad_fgain = norm_back(grad_normed)
    grad_stream = out_cotangent[0].astype(F32) + grad_before
    m_rows = gather(grad_stream.astype(BF), TP)
    output = before_forward + scatter_sum(dot(hidden, w_down, NT), TP)
    grad_rest = jnp.concatenate(
        [dot(m_rows, mixed, TN), dot(forward_rows, grad_gu, TN), dot(g_rows, hidden, TN)], 1
    )
    own_rest = scatter_sum(grad_rest, DP)

    d_qk, d_vg, d_bd, grad_cqk, grad_cv, grad_dlog, grad_dbias, grad_ogain = core_back(dot(m_rows, w_out))
    d_in = jnp.concatenate([d_qk.astype(BF), d_vg.astype(BF), d_bd.astype(BF)], 1)
    grad_normed = scatter_sum(dot(d_in, w_in, NT), TP)
    own_in = scatter_sum(dot(rows, d_in, TN), DP)
    _, norm_back = jax.vjp(norm_rows, stream, mixer_gain[0])
    grad_before, grad_mgain = norm_back(grad_normed)
    input_grad = grad_stream + grad_before

    heads = lax.psum((grad_cqk, grad_cv, grad_dlog, grad_dbias), DP)
    gains = lax.psum(jnp.concatenate([grad_mgain, grad_fgain, grad_ogain]), (DP, TP))
    d = grad_mgain.shape[0]
    return (
        output[None],
        input_grad[None],
        gains[None, :d],
        own_in[None, :, None, :nqk],
        own_in[None, :, None, nqk : nqk + nvg],
        own_in[None, :, None, nqk + nvg :],
        heads[0][None, :, None],
        heads[1][None, :, None],
        heads[2][None, None],
        heads[3][None, None],
        gains[None, 2 * d :],
        own_rest[:, :nout].T[None, None],
        gains[None, d : 2 * d],
        own_rest[:, nout : nout + 2 * ff].reshape(1, -1, 2, ff),
        own_rest[:, nout + 2 * ff :].T[None],
    )


def solution(mesh):
    placed = (
        P("dp", "tensor", None),
        P(),
        P(None, "dp", "tensor", None),
        P(None, "dp", "tensor", None),
        P(None, "dp", "tensor", None),
        P(None, None, "tensor", None),
        P(None, None, "tensor", None),
        P(None, "tensor"),
        P(None, "tensor"),
        P(),
        P(None, "tensor", None, "dp"),
        P(),
        P(None, "dp", None, "tensor"),
        P(None, "tensor", "dp"),
        P("dp", "tensor", None),
    )
    return jax.shard_map(
        body,
        mesh=mesh,
        in_specs=placed,
        out_specs=(
            P("dp", "tensor", None),
            P("dp", "tensor", None),
            P(),
            P(None, "dp", "tensor", None),
            P(None, "dp", "tensor", None),
            P(None, "dp", "tensor", None),
            P(None, None, "tensor", None),
            P(None, None, "tensor", None),
            P(None, "tensor"),
            P(None, "tensor"),
            P(),
            P(None, "tensor", None, "dp"),
            P(),
            P(None, "dp", None, "tensor"),
            P(None, "tensor", "dp"),
        ),
        check_vma=False,
    )
```

```python
import functools

import jax
import jax.numpy as jnp
from jax import lax
from jax.experimental import pallas as pl
from jax.experimental.pallas import tpu as pltpu
from jax.sharding import Mesh
from jax.sharding import PartitionSpec as P
C = 128
F32 = jnp.float32
BF = jnp.bfloat16
EPS = 1e-06
GATED_EPS = 1e-05
AXES = ("ylo", "x", "core", "yhi", "z")
MESH_ID = pl.DeviceIdType.MESH
ROWS = 128
HALF = 64


class Place:
    def __init__(self):
        self.ylo, self.x, self.core, self.yhi, self.z = (lax.axis_index(a) for a in AXES)
        self.same = self.core == self.yhi
        self.block = self.core * 4 + self.z

    def at(self, **other):
        return {a: other.get(a, getattr(self, a)) for a in AXES}

    def sibling(self):
        return self.at(core=1 - self.core)

    def right(self):
        return self.at(z=lax.rem(self.z + 1, 4))

    def left(self):
        return self.at(z=lax.rem(self.z + 3, 4))

    def swapped(self):
        return self.at(core=self.yhi, yhi=self.core)

    def plane(self, i, j, m, flip):
        core, yhi = self.yhi, self.core
        if m and flip == "yhi":
            yhi = 1 - yhi
        if m and flip == "core":
            core = 1 - core
        return self.at(ylo=lax.rem(self.ylo + i, 2), x=lax.rem(self.x + j, 4), core=core, yhi=yhi)


OFFSETS = [(i, j, m) for i in range(2) for j in range(4) for m in range(2)]


def greet(place, ring, plane_sources, tensor_peers=False):
    bar = pltpu.get_barrier_semaphore()
    count = 0

    def say(device):
        pl.semaphore_signal(bar, inc=1, device_id=device, device_id_type=MESH_ID)

    if ring:
        for device in (place.sibling(), place.right(), place.left()):
            say(device)
        count += 3
    if tensor_peers:
        for device in peers_of(place):
            say(device)
        count += 7
    if plane_sources:
        for flip in plane_sources:
            for i, j, m in OFFSETS[1:]:
                say(place.plane(i, j, m, flip))
            count += 15

        @pl.when(jnp.logical_not(place.same))
        def _():
            say(place.swapped())

        count = count + jnp.where(place.same, 0, 1)
    pl.semaphore_wait(bar, count)


def remote(src, dst, sems, i, device):
    return pltpu.make_async_remote_copy(
        src_ref=src, dst_ref=dst, send_sem=sems.at[0, i], recv_sem=sems.at[1, i], device_id=device, device_id_type=MESH_ID
    )


class Swap:
    def __init__(self, place, src, dst, sems, i):
        self.place = place
        self.copy = remote(src, dst, sems, i, place.swapped())
        self.own = pltpu.make_async_copy(src, dst, sems.at[0, i])

    def start(self):
        pl.when(self.place.same)(self.own.start)
        pl.when(jnp.logical_not(self.place.same))(self.copy.start)

    def wait(self):
        pl.when(self.place.same)(self.own.wait)
        pl.when(jnp.logical_not(self.place.same))(self.copy.wait)


class Plane:
    def __init__(self, place, gather, src, dst, sems):
        self.place = place
        flip = "yhi" if gather else "core"
        mine = (place.ylo * 4 + place.x) * 2 + (place.core if gather else place.yhi)
        self.copies, self.arrivals = [], []
        for n, (i, j, m) in enumerate(OFFSETS):
            target = place.plane(i, j, m, flip)
            index = (target["ylo"] * 4 + target["x"]) * 2 + target["core"]
            part = src if gather else src.at[index]
            copy = pltpu.make_async_remote_copy(
                src_ref=part, dst_ref=dst.at[mine], send_sem=sems.at[0, n], recv_sem=sems.at[1, mine],
                device_id=target, device_id_type=MESH_ID,
            )
            other = place.yhi if gather else place.core
            slot = (lax.rem(place.ylo + i, 2) * 4 + lax.rem(place.x + j, 4)) * 2 + lax.rem(other + m, 2)
            arrival = pltpu.make_async_remote_copy(
                src_ref=part, dst_ref=dst.at[slot], send_sem=sems.at[0, n], recv_sem=sems.at[1, slot],
                device_id=target, device_id_type=MESH_ID,
            )
            self.copies.append(copy)
            self.arrivals.append(arrival)
            if n == 0:
                self.own = pltpu.make_async_copy(part, dst.at[mine], sems.at[0, 0])

    def start(self):
        pl.when(self.place.same)(self.own.start)
        pl.when(jnp.logical_not(self.place.same))(self.copies[0].start)
        for copy in self.copies[1:]:
            copy.start()

    def wait(self):
        pl.when(self.place.same)(self.own.wait)

        @pl.when(jnp.logical_not(self.place.same))
        def _():
            self.copies[0].wait_send()
            self.arrivals[0].wait_recv()

        for copy, arrival in zip(self.copies[1:], self.arrivals[1:]):
            copy.wait_send()
            arrival.wait_recv()


class Gather:
    def __init__(self, place, own, full, sems):
        p = self.place = place

        def rows(z, lo=0, n=ROWS):
            return full.at[pl.ds(pl.multiple_of((p.core * 4 + lax.rem(z, 4)) * ROWS + lo, HALF), n)]

        here, left, right = rows(p.z), rows(p.z + 3), rows(p.z + 1)
        far_lo, far_hi = rows(p.z + 2, 0, HALF), rows(p.z + 2, HALF, HALF)
        left_lo, right_hi = rows(p.z + 3, 0, HALF), rows(p.z + 1, HALF, HALF)
        sib = p.sibling()
        self.keep = pltpu.make_async_copy(own, here, sems.at[0, 9])
        self.c = [
            remote(own, here, sems, 0, p.right()),
            remote(own, here, sems, 1, p.left()),
            remote(own, here, sems, 2, sib),
            remote(left_lo, left_lo, sems, 3, p.right()),
            remote(right_hi, right_hi, sems, 4, p.left()),
            remote(left, left, sems, 5, sib),
            remote(right, right, sems, 6, sib),
            remote(far_lo, far_lo, sems, 7, sib),
            remote(far_hi, far_hi, sems, 8, sib),
        ]

    def start(self):
        self.keep.start()
        for i in (0, 1, 2):
            self.c[i].start()

    def middle(self):
        self.c[0].wait_recv()
        self.c[3].start()
        self.c[1].wait_recv()
        self.c[4].start()
        self.c[5].start()
        self.c[6].start()

    def late(self):
        self.c[3].wait_recv()
        self.c[7].start()
        self.c[4].wait_recv()
        self.c[8].start()

    def finish(self):
        self.keep.wait()
        for i in (0, 1, 3, 4):
            self.c[i].wait_send()
        for i in (2, 5, 6, 7, 8):
            self.c[i].wait()

    def run(self):
        self.start()
        self.middle()
        self.late()
        self.finish()


class Scatter:
    def __init__(self, place, terms, scratch, sems):
        p = self.place = place
        self.here, self.there, self.out, self.near, self.ends = scratch
        z = p.z
        self.order = [lax.rem(z + 2, 4), lax.rem(z + 1, 4), lax.rem(z + 3, 4), z]

        def rows(core, zz):
            return terms.at[pl.ds(pl.multiple_of((core * 4 + zz) * ROWS, ROWS), ROWS)]

        sib, right, left = p.sibling(), p.right(), p.left()
        self.cross, self.load = [], []
        for n, zz in enumerate(self.order):
            self.cross.append(remote(rows(1 - p.core, zz), self.there.at[n], sems, n, sib))
            self.load.append(pltpu.make_async_copy(rows(p.core, zz), self.here.at[n], sems.at[0, 10 + n]))
        lo, hi = pl.ds(0, HALF), pl.ds(HALF, HALF)
        out, near, ends = self.out, self.near, self.ends
        self.far_lo = remote(out.at[0, lo], near.at[0], sems, 4, right)
        self.far_hi = remote(out.at[0, hi], near.at[1], sems, 5, left)
        self.right_hi = remote(out.at[1, hi], ends.at[0, hi], sems, 6, right)
        self.left_lo = remote(out.at[2, lo], ends.at[1, lo], sems, 7, left)
        self.right_lo = remote(out.at[1, lo], ends.at[0, lo], sems, 8, right)
        self.left_hi = remote(out.at[2, hi], ends.at[1, hi], sems, 9, left)

    def start(self):
        for a, b in zip(self.cross, self.load):
            a.start()
            b.start()

    def pair(self, n, rows=slice(None)):
        return self.here[n, rows].astype(F32) + self.there[n, rows].astype(F32)

    def arrived(self, n):
        self.load[n].wait()
        self.cross[n].wait()

    def middle(self):
        self.arrived(0)
        self.out[0] = self.pair(0).astype(BF)
        self.far_lo.start()
        self.far_hi.start()
        lo, hi = slice(0, HALF), slice(HALF, ROWS)
        self.arrived(1)
        self.out[1, hi] = self.pair(1, hi).astype(BF)
        self.right_hi.start()
        self.arrived(2)
        self.out[2, lo] = self.pair(2, lo).astype(BF)
        self.left_lo.start()
        self.arrived(3)

    def late(self):
        lo, hi = slice(0, HALF), slice(HALF, ROWS)
        self.far_lo.wait_recv()
        self.out[1, lo] = (self.pair(1, lo) + self.near[0].astype(F32)).astype(BF)
        self.right_lo.start()
        self.far_hi.wait_recv()
        self.out[2, hi] = (self.pair(2, hi) + self.near[1].astype(F32)).astype(BF)
        self.left_hi.start()

    def finish(self):
        for c in (self.right_hi, self.left_lo, self.right_lo, self.left_hi):
            c.wait()
        self.far_lo.wait_send()
        self.far_hi.wait_send()
        return self.pair(3) + self.ends[0].astype(F32) + self.ends[1].astype(F32)

    def run(self):
        self.start()
        self.middle()
        self.late()
        return self.finish()


def scatter_scratch(d):
    return [
        pltpu.VMEM((4, ROWS, d), BF),
        pltpu.VMEM((4, ROWS, d), BF),
        pltpu.VMEM((3, ROWS, d), BF),
        pltpu.VMEM((2, HALF, d), BF),
        pltpu.VMEM((2, ROWS, d), BF),
    ]


GATHER_SEMS = pltpu.SemaphoreType.DMA((2, 10))
SCATTER_SEMS = pltpu.SemaphoreType.DMA((2, 14))
PLANE_SEMS = pltpu.SemaphoreType.DMA((2, 16))


def peers_of(place):
    return [
        place.at(yhi=lax.rem(place.yhi + i, 2), z=lax.rem(place.z + j, 4)) for i in range(2) for j in range(4) if i or j
    ]


def normed(x, gain):
    return x * lax.rsqrt(jnp.mean(x * x, -1, keepdims=True) + EPS) * gain


def norm_back(x, gain, grad):
    r = lax.rsqrt(jnp.mean(x * x, -1, keepdims=True) + EPS)
    weighted = gain * grad
    by_x = r * weighted - x * (r * r * r) * jnp.mean(x * weighted, -1, keepdims=True)
    return by_x, jnp.sum(grad * x * r, 0, keepdims=True)


def entry_kernel(x_ref, g_ref, gain_ref, head_ref, w_ref, xs_ref, gs_ref, heads_ref, wall_ref, rows_ref,
                 own, sw_sems, pl_sems, ga_sems):
    place = Place()
    greet(place, True, ("core",))
    swaps = [Swap(place, a, b, sw_sems, i) for i, (a, b) in enumerate(((x_ref, xs_ref), (g_ref, gs_ref), (head_ref, heads_ref)))]
    weights = Plane(place, True, w_ref, wall_ref, pl_sems)
    swaps[0].start()
    swaps[2].start()
    weights.start()
    swaps[1].start()
    swaps[0].wait()
    own[...] = normed(xs_ref[...].astype(F32), gain_ref[...]).astype(BF)
    Gather(place, own, rows_ref, ga_sems).run()
    swaps[1].wait()
    swaps[2].wait()
    weights.wait()


def sum_norm_gather_kernel(terms_ref, x_ref, gain_ref, stream_ref, rows_ref, own, here, there, out, near, ends, sc_sems, ga_sems):
    place = Place()
    greet(place, True, ())
    stream = x_ref[...].astype(F32) + Scatter(place, terms_ref, (here, there, out, near, ends), sc_sems).run()
    stream_ref[...] = stream
    own[...] = normed(stream, gain_ref[...]).astype(BF)
    Gather(place, own, rows_ref, ga_sems).run()


def sum_back_gather_kernel(terms_ref, stream_ref, gain_ref, g_ref, grad_ref, dgain_ref, rows_ref, own, here, there, out,
                           near, ends, sc_sems, ga_sems):
    place = Place()
    greet(place, True, ())
    grad = Scatter(place, terms_ref, (here, there, out, near, ends), sc_sems).run()
    by_x, by_gain = norm_back(stream_ref[...], gain_ref[...], grad)
    grad = g_ref[...].astype(F32) + by_x
    grad_ref[...] = grad
    own[...] = grad.astype(BF)
    ring = Gather(place, own, rows_ref, ga_sems)
    ring.start()
    dgain_ref[...] = by_gain
    ring.middle()
    ring.late()
    ring.finish()


def exit_kernel(terms_ref, x_ref, gain_ref, grad_ref, output_ref, dw_ref, small_ref, final_ref, input_ref, parts_ref, sums_ref,
                own, here, there, out, near, ends, mine, plane_sums, total, peer_sums, sc_sems, sw_sems, pl_sems, sm_sems, pe_sems):
    place = Place()
    greet(place, True, ("yhi",), True)
    d = gain_ref.shape[1]
    swap_output = Swap(place, output_ref, final_ref, sw_sems, 0)
    swap_output.start()
    ring = Scatter(place, terms_ref, (here, there, out, near, ends), sc_sems)
    ring.start()
    weights = Plane(place, False, dw_ref, parts_ref, pl_sems)
    weights.start()
    ring.middle()
    ring.late()
    grad = ring.finish()
    by_x, by_gain = norm_back(x_ref[...].astype(F32), gain_ref[...], grad)
    own[...] = (grad_ref[...] + by_x).astype(BF)
    swap_input = Swap(place, own, input_ref, sw_sems, 1)
    swap_input.start()
    mine[...] = small_ref[...]
    for i in range(d // 128):
        mine[i : i + 1, :] = by_gain[:, i * 128 : (i + 1) * 128]
    small = PlaneSame(place, mine, plane_sums, sm_sems)
    small.start()
    small.wait()
    subtotal = plane_sums[0]
    for i in range(1, 16):
        subtotal = subtotal + plane_sums[i]
    total[...] = subtotal
    n = peer_sums.shape[1]
    copies = [
        remote(total.at[pl.ds(0, n)], peer_sums.at[i], pe_sems, i, device) for i, device in enumerate(peers_of(place))
    ]
    for copy in copies:
        copy.start()
    sums_ref[...] = subtotal
    for copy in copies:
        copy.wait()
    gains = subtotal[:n]
    for i in range(7):
        gains = gains + peer_sums[i]
    sums_ref[0:n, :] = gains
    weights.wait()
    swap_output.wait()
    swap_input.wait()


class PlaneSame(Plane):
    def __init__(self, place, src, dst, sems):
        Plane.__init__(self, place, False, Same(src), dst, sems)


class Same:
    def __init__(self, ref):
        self.ref = ref
        self.at = self

    def __getitem__(self, index):
        return self.ref


HI = lax.Precision.HIGHEST
LO = lax.Precision.DEFAULT
NN = (((1,), (0,)), ((), ()))
NT = (((1,), (1,)), ((), ()))
TN = (((0,), (0,)), ((), ()))


def mm(a, b, dims=NN, precision=HI):
    return lax.dot_general(a, b, dims, precision=precision, preferred_element_type=F32)


def chunk_masks():
    row = lax.broadcasted_iota(jnp.int32, (C, C), 0)
    col = lax.broadcasted_iota(jnp.int32, (C, C), 1)
    return row, col


def decay_parts(g, row, col):
    lower = (row >= col).astype(F32)
    cum = mm(lower, g)
    table = jnp.where(row >= col, jnp.exp(jnp.where(row >= col, cum - cum.T, 0.0)), 0.0)
    last = cum[C - 1 : C, :]
    return table, jnp.exp(cum), jnp.exp(last - cum), jnp.exp(last)


def wide(x):
    return jnp.concatenate([x, x], axis=1)


def inverse_many(systems, row, col, prec):
    eye = (row == col).astype(F32)
    near = (row // 8) == (col // 8)
    a1 = [jnp.where(near, a, 0.0) for a in systems]
    a2 = [mm(a, a, precision=prec) for a in a1]
    x = [eye - a for a in a1]
    a4 = [mm(a, a, precision=prec) for a in a2]
    x = [y + mm(y, a, precision=prec) for y, a in zip(x, a2)]
    x = [y + mm(y, a, precision=prec) for y, a in zip(x, a4)]
    size = 8
    while size < C:
        pick = ((row // (2 * size)) == (col // (2 * size))) & ((row // size) != (col // size))
        off = [jnp.where(pick, a, 0.0) for a in systems]
        y = [mm(o, t, precision=prec) for o, t in zip(off, x)]
        x = [t - mm(t, z, precision=prec) for t, z in zip(x, y)]
        size *= 2
    return x


def fwd_kernel(P_, group, q_ref, k_ref, v_ref, b_ref, g_ref, grow_ref, shard_ref, o_ref, t_ref, u_ref, s_ref, f_ref, w_ref,
               grows_ref, wall_ref, z_ref, pl_sems, ga_sems):
    place = Place()
    greet(place, True, ("core",))
    weights = Plane(place, True, shard_ref, wall_ref, pl_sems)
    ring = Gather(place, grow_ref, grows_ref, ga_sems)
    weights.start()
    ring.start()
    nb = q_ref.shape[0] // C
    row, col = chunk_masks()

    def first(i, _):
        cs = [pl.ds(pl.multiple_of((i * group + j) * C, C), C) for j in range(group)]
        q = [q_ref[c, :] for c in cs]
        k = [k_ref[c, :] for c in cs]
        v = [v_ref[c, :] for c in cs]
        b = [b_ref[c, :] for c in cs]
        parts = [decay_parts(g_ref[c, :], row, col) for c in cs]
        kk = [mm(x, x, NT, P_["kk"]) for x in k]
        system = [jnp.where(row > col, bb * x * p[0], 0.0) for bb, x, p in zip(b, kk, parts)]
        t = inverse_many(system, row, col, P_["inv"])
        w = [mm(tt, bb * p[1] * x, precision=P_["w"]) for tt, bb, p, x in zip(t, b, parts, k)]
        u0 = [mm(tt, wide(bb) * x, precision=P_["u"]) for tt, bb, x in zip(t, b, v)]
        kd = [x * p[2] for x, p in zip(k, parts)]
        eye = (row == col).astype(F32)
        for c, kdd, ww, uu, tt, p in zip(cs, kd, w, u0, t, parts):
            t_ref[c, :] = tt
            w_ref[c, :] = ww
            u_ref[c, :] = uu
            f_ref[c, :] = eye * p[3] - mm(kdd, ww, TN, P_["f"])
            z_ref[c, :] = mm(kdd, uu, TN, P_["z"])
        return 0

    lax.fori_loop(0, nb // group, first, 0)
    ring.middle()
    state = jnp.zeros((C, v_ref.shape[1]), F32)
    for i in range(nb):
        c = pl.ds(i * C, C)
        s_ref[c, :] = state
        if i < nb - 1:
            state = z_ref[c, :] + mm(f_ref[c, :], state, precision=P_["chain"])
    ring.late()

    def last(i, _):
        cs = [pl.ds(pl.multiple_of((i * group + j) * C, C), C) for j in range(group)]
        for c in cs:
            q, k, s = q_ref[c, :], k_ref[c, :], s_ref[c, :]
            table, scale, _, _ = decay_parts(g_ref[c, :], row, col)
            u = u_ref[c, :] - mm(w_ref[c, :], s, precision=P_["ws"])
            u_ref[c, :] = u
            scores = mm(q, k, NT, P_["qk"]) * table
            o_ref[c, :] = mm(q * scale, s, precision=P_["o"]) + mm(scores, u, precision=P_["o"])
        return 0

    lax.fori_loop(0, nb // group, last, 0)
    ring.finish()
    weights.wait()


def bwd_kernel(P_, group, q_ref, k_ref, v_ref, b_ref, g_ref, t_ref, u_ref, s_ref, f_ref, w_ref, do_ref,
               terms_ref, stream_ref, dw_ref, dq_ref, dk_ref, dv_ref, db_ref, dg_ref, output_ref, parts_ref, ds_ref, x_ref,
               here, there, out, near, ends, sc_sems, pl_sems):
    place = Place()
    greet(place, True, ("yhi",))
    ring = Scatter(place, terms_ref, (here, there, out, near, ends), sc_sems)
    weights = Plane(place, False, dw_ref, parts_ref, pl_sems)
    ring.start()
    weights.start()
    nb = q_ref.shape[0] // C
    row, col = chunk_masks()

    def first(i, _):
        cs = [pl.ds(pl.multiple_of((i * group + j) * C, C), C) for j in range(group)]
        for c in cs:
            q, k, do = q_ref[c, :], k_ref[c, :], do_ref[c, :]
            table, scale, _, _ = decay_parts(g_ref[c, :], row, col)
            scores = mm(q, k, NT, P_["qk"]) * table
            x = mm(scores, do, TN, P_["bx"])
            x_ref[c, :] = x
            ds_ref[c, :] = mm(q * scale, do, TN, P_["bx"]) - mm(w_ref[c, :], x, TN, P_["bx"])
        return 0

    lax.fori_loop(0, nb // group, first, 0)
    ring.middle()
    carry = jnp.zeros((C, v_ref.shape[1]), F32)
    for i in reversed(range(nb)):
        c = pl.ds(i * C, C)
        own = ds_ref[c, :]
        ds_ref[c, :] = carry
        if i > 0:
            carry = own + mm(f_ref[c, :], carry, TN, P_["chain"])
    ring.late()

    def last(i, _):
        cs = [pl.ds(pl.multiple_of((i * group + j) * C, C), C) for j in range(group)]
        for c in cs:
            q, k, v, b, do = q_ref[c, :], k_ref[c, :], v_ref[c, :], b_ref[c, :], do_ref[c, :]
            t, u, s, ds = t_ref[c, :], u_ref[c, :], s_ref[c, :], ds_ref[c, :]
            table, scale, tail, total = decay_parts(g_ref[c, :], row, col)
            p = P_["bl"]
            qk = mm(q, k, NT, p)
            kk = mm(k, k, NT, p)
            ks = mm(k, s, precision=p)
            qs = mm(q, s, precision=p)
            kd = k * tail
            du = x_ref[c, :] + mm(kd, ds, precision=p)
            dr = mm(t, du, TN, P_["bt"])
            dp = jnp.where(row >= col, mm(do, u, NT, p), 0.0)
            da = jnp.where(row > col, -mm(dr, u, NT, p), 0.0)
            dqk = dp * table
            dkk = da * b * table
            n = dqk * qk + dkk * kk
            dkd = mm(u, ds, NT, p)
            dq_ref[c, :] = scale * mm(do, s, NT, p) + mm(dqk, k, precision=p)
            bdr = wide(b) * dr
            dk_ref[c, :] = (
                mm(dqk, q, TN, p)
                + mm(dkk, k, precision=p)
                + mm(dkk, k, TN, p)
                + dkd * tail
                - scale * mm(bdr, s, NT, p)
            )
            dv_ref[c, :] = bdr
            sc2 = wide(scale)
            db = jnp.sum(dr * (v - sc2 * ks), 1, keepdims=True) + jnp.sum(da * table * kk, 1, keepdims=True)
            db_ref[c, :] = jnp.broadcast_to(db, (C, C))
            tails = jnp.sum(dkd * kd, 1, keepdims=True)
            dcum = (
                jnp.sum(n, 1, keepdims=True)
                - jnp.sum(n.T, 1, keepdims=True)
                + jnp.sum(sc2 * (do * qs - bdr * ks), 1, keepdims=True)
                - tails
            )
            dcum = jnp.broadcast_to(dcum, (C, C))
            extra = jnp.sum(tails) + jnp.sum(ds * s * wide(jnp.broadcast_to(total, (C, C))))
            upper = (row <= col).astype(F32)
            dg_ref[c, :] = mm(upper, dcum) + extra
        return 0

    lax.fori_loop(0, nb // group, last, 0)
    output_ref[...] = (stream_ref[...] + ring.finish()).astype(BF)
    weights.wait()


KEYS = ("kk", "inv", "w", "u", "f", "z", "chain", "ws", "qk", "o", "bx", "bl", "bt")
PRECS = {key: HI for key in KEYS}
VM = pl.BlockSpec(memory_space=pltpu.VMEM)
ANY = pl.BlockSpec(memory_space=pl.ANY)


def call(kernel, name, number, ins, in_specs, outs, out_specs, scratch):
    return pl.pallas_call(
        kernel,
        name=name,
        out_shape=[jax.ShapeDtypeStruct(s, t) for s, t in outs],
        in_specs=in_specs,
        out_specs=out_specs,
        scratch_shapes=scratch,
        compiler_params=pltpu.CompilerParams(
            collective_id=number, has_side_effects=True, vmem_limit_bytes=48 * 2**20
        ),
    )(*ins)


def causal_conv(inputs, taps):
    length = inputs.shape[0]
    padded = jnp.pad(inputs, ((taps.shape[0] - 1, 0), (0, 0)))
    summed = padded[0:length] * taps[0]
    for shift_at in range(1, taps.shape[0]):
        summed = summed + padded[shift_at : shift_at + length] * taps[shift_at]
    return summed


def before_delta(qk_pre, v_pre, bd_pre, conv_qk, conv_v, decay_log, decay_bias):
    dk = qk_pre.shape[-1] // 2
    rows = jax.nn.silu(causal_conv(qk_pre, conv_qk))
    q, k = rows[:, :dk], rows[:, dk:]
    q = q * lax.rsqrt(jnp.sum(q * q, -1, keepdims=True) + EPS) * dk ** (-0.5)
    k = k * lax.rsqrt(jnp.sum(k * k, -1, keepdims=True) + EPS)
    v = jax.nn.silu(causal_conv(v_pre, conv_v))
    b = jax.nn.sigmoid(bd_pre[:, 0])
    g = -jnp.exp(decay_log) * jax.nn.softplus(bd_pre[:, 1] + decay_bias)
    return q, k, v, jnp.broadcast_to(b[:, None], (b.shape[0], C)), jnp.broadcast_to(g[:, None], (g.shape[0], C))


def after_delta(delta_out, gates, gain):
    r = lax.rsqrt(jnp.mean(delta_out * delta_out, -1, keepdims=True) + GATED_EPS)
    return delta_out * r * gain * jax.nn.silu(gates)


def dot(a, b, dims=NN):
    return lax.dot_general(a, b, dims, preferred_element_type=F32)


def padded(x, width):
    return jnp.pad(x, ((0, 0), (0, width - x.shape[1])))


def up_to(n, k):
    return -(-n // k) * k


def body(
    block_input,
    mixer_gain,
    query_key_weight,
    value_gate_weight,
    beta_decay_weight,
    conv_query_key,
    conv_value,
    decay_log,
    decay_bias,
    out_gain,
    out_weight,
    forward_gain,
    gate_up_weight,
    down_weight,
    out_cotangent,
):
    d = block_input.shape[2]
    n = block_input.shape[1] * 8
    nqk, nvg, nbd = query_key_weight.shape[-1], value_gate_weight.shape[-1], beta_decay_weight.shape[-1]
    ff = gate_up_weight.shape[-1]
    dv = out_weight.shape[2]
    own_d = query_key_weight.shape[1]
    wide_in, wide_rest = up_to(nqk + nvg + nbd, 128), up_to(dv + 3 * ff, 128)
    first_pack = padded(
        jnp.concatenate([query_key_weight[0, :, 0], value_gate_weight[0, :, 0], beta_decay_weight[0, :, 0]], 1), wide_in
    )
    second_pack = padded(
        jnp.concatenate([out_weight[0, 0].T, gate_up_weight[0].reshape(-1, 2 * ff), down_weight[0].T], 1), wide_rest
    )
    taps = conv_query_key.shape[1]
    heads = jnp.concatenate(
        [
            conv_query_key[0, :, 0].reshape(-1, 128),
            conv_value[0, :, 0].reshape(-1, 128),
            padded(jnp.concatenate([decay_log, decay_bias], 1), 128),
        ]
    )
    head_rows = up_to(heads.shape[0], 8)
    heads = jnp.pad(heads, ((0, head_rows - heads.shape[0]), (0, 0)))
    sems = pltpu.SemaphoreType.DMA
    block = (ROWS, d)

    x, g, heads, w_in, rows = call(
        entry_kernel,
        "entry_exchange",
        0,
        (block_input[0], out_cotangent[0], mixer_gain, heads, first_pack),
        [VM, VM, VM, VM, ANY],
        [(block, BF), (block, BF), (heads.shape, F32), ((16, own_d, wide_in), BF), ((n, d), BF)],
        [VM, VM, VM, ANY, ANY],
        [pltpu.VMEM(block, BF), sems((2, 3)), PLANE_SEMS, GATHER_SEMS],
    )
    w_in = w_in.reshape(d, wide_in)
    size = taps * nqk // 128
    conv_qk, conv_v = heads[:size].reshape(taps, nqk), heads[size : 2 * size].reshape(taps, dv)
    decays = heads[2 * size]

    pre = dot(rows, w_in)
    gates = pre[:, nqk + dv : nqk + nvg]
    (q, k, v, b, ld), pre_back = jax.vjp(
        before_delta, pre[:, :nqk], pre[:, nqk : nqk + dv], pre[:, nqk + nvg :], conv_qk, conv_v, decays[0], decays[1]
    )
    f = lambda width: ((n, width), F32)
    delta_out, t, u, s, fm, w, g_rows, w_rest = call(
        functools.partial(fwd_kernel, PRECS, 4),
        "delta_forward",
        1,
        (q, k, v, b, ld, g, second_pack),
        [VM] * 5 + [ANY] * 2,
        [f(dv), f(C), f(dv), f(dv), f(C), f(C), ((n, d), BF), ((16, own_d, wide_rest), BF)],
        [VM] * 6 + [ANY] * 2,
        [pltpu.VMEM((n, dv), F32), PLANE_SEMS, GATHER_SEMS],
    )
    w_rest = w_rest.reshape(d, wide_rest)
    w_out, w_gu, w_down = w_rest[:, :dv], w_rest[:, dv : dv + 2 * ff], w_rest[:, dv + 2 * ff : dv + 3 * ff]
    mixed, post_back = jax.vjp(after_delta, delta_out, gates, out_gain)
    mixed = mixed.astype(BF)
    stream, forward_rows = call(
        sum_norm_gather_kernel,
        "sum_norm_gather",
        2,
        (dot(mixed, w_out, NT).astype(BF), x, forward_gain),
        [ANY, VM, VM],
        [(block, F32), ((n, d), BF)],
        [VM, ANY],
        [pltpu.VMEM(block, BF)] + scatter_scratch(d) + [SCATTER_SEMS, GATHER_SEMS],
    )
    gate = dot(forward_rows, w_gu[:, :ff])
    up = dot(forward_rows, w_gu[:, ff:])
    sg = jax.nn.sigmoid(gate)
    hidden = (gate * sg * up).astype(BF)
    grad_hidden = dot(g_rows, w_down)
    grad_gu = jnp.concatenate(
        [(grad_hidden * up * sg * (1.0 + gate * (1.0 - sg))).astype(BF), (grad_hidden * gate * sg).astype(BF)], 1
    )
    grad_stream, grad_fgain, m_rows = call(
        sum_back_gather_kernel,
        "sum_back_gather",
        3,
        (dot(grad_gu, w_gu, NT).astype(BF), stream, forward_gain, g),
        [ANY, VM, VM, VM],
        [(block, F32), ((1, d), F32), ((n, d), BF)],
        [VM, VM, ANY],
        [pltpu.VMEM(block, BF)] + scatter_scratch(d) + [SCATTER_SEMS, GATHER_SEMS],
    )
    grad_rest = padded(
        jnp.concatenate([dot(m_rows, mixed, TN), dot(forward_rows, grad_gu, TN), dot(g_rows, hidden, TN)], 1).astype(BF),
        wide_rest,
    ).reshape(16, own_d, wide_rest)
    grad_delta, grad_gates, grad_ogain = post_back(dot(m_rows, w_out))
    dq, dk, dvalue, db, dg, output, rest_parts = call(
        functools.partial(bwd_kernel, PRECS, 2),
        "delta_backward",
        4,
        (q, k, v, b, ld, t, u, s, fm, w, grad_delta, dot(hidden, w_down, NT).astype(BF), stream, grad_rest),
        [VM] * 11 + [ANY, VM, ANY],
        [f(C), f(C), f(dv), f(C), f(C), (block, BF), ((16, own_d, wide_rest), BF)],
        [VM] * 6 + [ANY],
        [pltpu.VMEM((n, dv), F32)] * 2 + scatter_scratch(d) + [SCATTER_SEMS, PLANE_SEMS],
    )
    share = 1.0 / C
    d_qk, d_v, d_bd, grad_cqk, grad_cv, grad_dlog, grad_dbias = pre_back((dq, dk, dvalue, db * share, dg * share))
    d_in = padded(jnp.concatenate([d_qk, d_v, grad_gates, d_bd], 1).astype(BF), wide_in)
    gain_rows = up_to((2 * d + dv) // 128, 8)
    zero = jnp.zeros((1, 128), F32)
    small = jnp.concatenate(
        [
            jnp.zeros((d // 128, 128), F32),
            grad_fgain.reshape(-1, 128),
            grad_ogain.reshape(-1, 128),
            jnp.zeros((gain_rows - (2 * d + dv) // 128, 128), F32),
            grad_cqk.reshape(-1, 128),
            grad_cv.reshape(-1, 128),
            padded(jnp.stack([grad_dlog, grad_dbias])[None], 128),
            jnp.zeros((head_rows - 2 * size - 1, 128), F32),
        ]
    )
    small_rows = small.shape[0]
    final, input_grad, in_parts, sums = call(
        exit_kernel,
        "exit_exchange",
        5,
        (
            dot(d_in, w_in, NT).astype(BF),
            x,
            mixer_gain,
            grad_stream,
            output,
            dot(rows, d_in, TN).astype(BF).reshape(16, own_d, wide_in),
            small,
        ),
        [ANY, VM, VM, VM, VM, ANY, VM],
        [(block, BF), (block, BF), ((16, own_d, wide_in), BF), ((small_rows, 128), F32)],
        [ANY, ANY, ANY, VM],
        [pltpu.VMEM(block, BF)]
        + scatter_scratch(d)
        + [
            pltpu.VMEM((small_rows, 128), F32),
            pltpu.VMEM((16, small_rows, 128), F32),
            pltpu.VMEM((small_rows, 128), F32),
            pltpu.VMEM((7, gain_rows, 128), F32),
            SCATTER_SEMS,
            sems((2, 2)),
            PLANE_SEMS,
            PLANE_SEMS,
            sems((2, 7)),
        ],
    )
    own_rest = jnp.sum(rest_parts.astype(F32), 0)
    own_in = jnp.sum(in_parts.astype(F32), 0)
    k8 = d // 128
    hs = sums[gain_rows:]
    return (
        final.astype(F32)[None],
        input_grad.astype(F32)[None],
        sums[:k8].reshape(1, d),
        own_in[None, :, None, :nqk],
        own_in[None, :, None, nqk : nqk + nvg],
        own_in[None, :, None, nqk + nvg : nqk + nvg + nbd],
        hs[:size].reshape(1, taps, 1, nqk),
        hs[size : 2 * size].reshape(1, taps, 1, dv),
        hs[2 * size : 2 * size + 1, :1],
        hs[2 * size : 2 * size + 1, 1:2],
        sums[2 * k8 : 2 * k8 + dv // 128].reshape(1, dv),
        own_rest[:, :dv].T[None, None],
        sums[k8 : 2 * k8].reshape(1, d),
        own_rest[:, dv : dv + 2 * ff].reshape(1, -1, 2, ff),
        own_rest[:, dv + 2 * ff : dv + 3 * ff].T[None],
    )


def solution(mesh):
    parts = Mesh(mesh.devices.reshape(2, 4, 2, 2, 4), AXES)
    dp, tp = ("ylo", "x", "core"), ("yhi", "z")
    stream = P(dp, tp, None)
    head = P(None, tp)
    proj = P(None, dp, tp, None)
    conv = P(None, None, tp, None)
    out_w, gu_w, down_w = P(None, tp, None, dp), P(None, dp, None, tp), P(None, tp, dp)
    return jax.shard_map(
        body,
        mesh=parts,
        in_specs=(stream, P(), proj, proj, proj, conv, conv, head, head, P(), out_w, P(), gu_w, down_w, stream),
        out_specs=(stream, stream, P(), proj, proj, proj, conv, conv, head, head, P(), out_w, P(), gu_w, down_w),
        check_vma=False,
    )
```

```python
import functools

import jax
import jax.numpy as jnp
from jax import lax
from jax.experimental import pallas as pl
from jax.experimental.pallas import tpu as pltpu
from jax.sharding import Mesh
from jax.sharding import PartitionSpec as P
C = 128
F32 = jnp.float32
BF = jnp.bfloat16
EPS = 1e-06
GATED_EPS = 1e-05
AXES = ("ylo", "x", "core", "yhi", "z")
MESH_ID = pl.DeviceIdType.MESH
ROWS = 128
HALF = 64


class Place:
    def __init__(self):
        self.ylo, self.x, self.core, self.yhi, self.z = (lax.axis_index(a) for a in AXES)
        self.same = self.core == self.yhi
        self.block = self.core * 4 + self.z

    def at(self, **other):
        return {a: other.get(a, getattr(self, a)) for a in AXES}

    def sibling(self):
        return self.at(core=1 - self.core)

    def right(self):
        return self.at(z=lax.rem(self.z + 1, 4))

    def left(self):
        return self.at(z=lax.rem(self.z + 3, 4))

    def swapped(self):
        return self.at(core=self.yhi, yhi=self.core)

    def plane(self, i, j, m, flip):
        core, yhi = self.yhi, self.core
        if m and flip == "yhi":
            yhi = 1 - yhi
        if m and flip == "core":
            core = 1 - core
        return self.at(ylo=lax.rem(self.ylo + i, 2), x=lax.rem(self.x + j, 4), core=core, yhi=yhi)


OFFSETS = [(i, j, m) for i in range(2) for j in range(4) for m in range(2)]


def greet(place, lines=(), swap=False, owners=False, tensor_peers=False):
    bar = pltpu.get_barrier_semaphore()
    count = 0
    devices = [place.sibling()]
    for axis in lines:
        line = Line(place, axis)
        devices += [line.device(i) for i in ((1, 3) if axis == "z" else (1, 2, 3))]
    if tensor_peers:
        devices += peers_of(place)
    if owners:
        devices += [place.plane(i, j, m, "yhi") for i, j, m in OFFSETS[1:]]
    for device in devices:
        pl.semaphore_signal(bar, inc=1, device_id=device, device_id_type=MESH_ID)
    count = len(devices)
    if swap or owners:

        @pl.when(jnp.logical_not(place.same))
        def _():
            pl.semaphore_signal(bar, inc=1, device_id=place.swapped(), device_id_type=MESH_ID)

        count = count + jnp.where(place.same, 0, 1)
    pl.semaphore_wait(bar, count)


def remote(src, dst, sems, i, device):
    return pltpu.make_async_remote_copy(
        src_ref=src, dst_ref=dst, send_sem=sems.at[0, i], recv_sem=sems.at[1, i], device_id=device, device_id_type=MESH_ID
    )


class Swap:
    def __init__(self, place, src, dst, sems, i):
        self.place = place
        self.copy = remote(src, dst, sems, i, place.swapped())
        self.own = pltpu.make_async_copy(src, dst, sems.at[0, i])

    def start(self):
        pl.when(self.place.same)(self.own.start)
        pl.when(jnp.logical_not(self.place.same))(self.copy.start)

    def wait(self):
        pl.when(self.place.same)(self.own.wait)
        pl.when(jnp.logical_not(self.place.same))(self.copy.wait)


class Plane:
    def __init__(self, place, gather, src, dst, sems):
        self.place = place
        flip = "yhi" if gather else "core"
        mine = (place.ylo * 4 + place.x) * 2 + (place.core if gather else place.yhi)
        self.copies, self.arrivals = [], []
        for n, (i, j, m) in enumerate(OFFSETS):
            target = place.plane(i, j, m, flip)
            index = (target["ylo"] * 4 + target["x"]) * 2 + target["core"]
            part = src if gather else src.at[index]
            copy = pltpu.make_async_remote_copy(
                src_ref=part, dst_ref=dst.at[mine], send_sem=sems.at[0, n], recv_sem=sems.at[1, mine],
                device_id=target, device_id_type=MESH_ID,
            )
            other = place.yhi if gather else place.core
            slot = (lax.rem(place.ylo + i, 2) * 4 + lax.rem(place.x + j, 4)) * 2 + lax.rem(other + m, 2)
            arrival = pltpu.make_async_remote_copy(
                src_ref=part, dst_ref=dst.at[slot], send_sem=sems.at[0, n], recv_sem=sems.at[1, slot],
                device_id=target, device_id_type=MESH_ID,
            )
            self.copies.append(copy)
            self.arrivals.append(arrival)
            if n == 0:
                self.own = pltpu.make_async_copy(part, dst.at[mine], sems.at[0, 0])

    def start(self):
        pl.when(self.place.same)(self.own.start)
        pl.when(jnp.logical_not(self.place.same))(self.copies[0].start)
        for copy in self.copies[1:]:
            copy.start()

    def wait(self):
        pl.when(self.place.same)(self.own.wait)

        @pl.when(jnp.logical_not(self.place.same))
        def _():
            self.copies[0].wait_send()
            self.arrivals[0].wait_recv()

        for copy, arrival in zip(self.copies[1:], self.arrivals[1:]):
            copy.wait_send()
            arrival.wait_recv()


class Line:
    def __init__(self, place, axis):
        self.place, self.axis = place, axis
        self.me = {"x": place.x, "z": place.z, "y": place.yhi * 2 + place.ylo}[axis]

    def index(self, i):
        return lax.rem(self.me + i, 4)

    def device(self, i):
        j = self.index(i)
        if self.axis == "y":
            return self.place.at(yhi=j // 2, ylo=lax.rem(j, 2))
        return self.place.at(**{self.axis: j})


class RingGather:
    def __init__(self, line, own, part, sems):
        here = part(line.me)
        self.keep = None
        if own is None:
            own = here
        else:
            self.keep = pltpu.make_async_copy(own, here, sems.at[0, 3])
        self.c = [remote(own, here, sems, i, line.device(i + 1)) for i in (1, 0, 2)]

    def start(self):
        if self.keep is not None:
            self.keep.start()
        for c in self.c:
            c.start()

    def finish(self):
        if self.keep is not None:
            self.keep.wait()
        for c in self.c:
            c.wait()


class RingSum:
    def __init__(self, line, part, ends, sems):
        self.own, self.ends = part(line.me), ends
        self.c = [remote(part(line.index(i + 1)), ends.at[i], sems, i, line.device(i + 1)) for i in (1, 0, 2)]

    def start(self):
        for c in self.c:
            c.start()

    def finish(self):
        for c in self.c:
            c.wait()
        total = self.own[...].astype(F32)
        for i in range(3):
            total = total + self.ends[i].astype(F32)
        return total.astype(BF)


class TwoWayGather:
    def __init__(self, line, own, part, sems):
        right, left = line.device(1), line.device(3)
        here = part(line.me, None)
        self.keep = None
        if own is None:
            own = here
        else:
            self.keep = pltpu.make_async_copy(own, here, sems.at[0, 4])
        from_left, from_right = part(line.index(3), 0), part(line.index(1), 1)
        self.c = [
            remote(own, here, sems, 0, right),
            remote(own, here, sems, 1, left),
            remote(from_left, from_left, sems, 2, right),
            remote(from_right, from_right, sems, 3, left),
        ]

    def start(self):
        if self.keep is not None:
            self.keep.start()
        self.c[0].start()
        self.c[1].start()

    def middle(self):
        self.c[0].wait_recv()
        self.c[2].start()
        self.c[1].wait_recv()
        self.c[3].start()

    def finish(self):
        if self.keep is not None:
            self.keep.wait()
        self.c[0].wait_send()
        self.c[1].wait_send()
        self.c[2].wait()
        self.c[3].wait()


class TwoWaySum:
    def __init__(self, line, part, scratch, sems):
        self.line, self.part = line, part
        self.near, self.out, self.ends = near, out, ends = scratch
        right, left = line.device(1), line.device(3)
        self.c = [
            remote(part(line.index(2), 0), near.at[0], sems, 0, right),
            remote(part(line.index(2), 1), near.at[1], sems, 1, left),
            remote(part(line.index(1), 1), ends.at[0, 1], sems, 2, right),
            remote(part(line.index(3), 0), ends.at[1, 0], sems, 3, left),
            remote(out.at[0], ends.at[0, 0], sems, 4, right),
            remote(out.at[1], ends.at[1, 1], sems, 5, left),
        ]

    def start(self):
        for i in range(4):
            self.c[i].start()

    def middle(self):
        line = self.line
        for i, (j, half) in enumerate(((line.index(1), 0), (line.index(3), 1))):
            self.c[i].wait_recv()
            self.out[i] = (self.part(j, half)[...].astype(F32) + self.near[i].astype(F32)).astype(BF)
            self.c[4 + i].start()

    def finish(self, take):
        self.c[0].wait_send()
        self.c[1].wait_send()
        for i in (2, 3, 4, 5):
            self.c[i].wait()
        for half in range(2):
            own = self.part(self.line.me, half)[...].astype(F32)
            take(half, (own + self.ends[0, half].astype(F32) + self.ends[1, half].astype(F32)).astype(BF))


class PlaneGather:
    def __init__(self, place, first, own, full, sems):
        def single(j):
            if first == "x":
                return full.at[place.ylo, j, place.yhi]
            return full.at[lax.rem(j, 2), place.x, j // 2]

        def whole(j, half):
            if first == "y":
                return full.at[:, j] if half is None else full.at[half, j]
            some = slice(None) if half is None else pl.ds(2 * half, 2)
            return full.at[lax.rem(j, 2), some, j // 2]

        self.one = RingGather(Line(place, first), own, single, sems.at[0])
        self.two = TwoWayGather(Line(place, "y" if first == "x" else "x"), None, whole, sems.at[1])

    def start(self):
        self.one.start()

    def middle(self):
        self.one.finish()
        self.two.start()

    def late(self):
        self.two.middle()

    def finish(self):
        self.two.finish()


class PlaneSum:
    def __init__(self, place, first, terms, scratch, own, sems):
        near, out, ends, partial, ends2 = scratch
        self.first, self.partial, self.own = first, partial, own

        def whole(j, half):
            if first == "x":
                return terms.at[half, j]
            return terms.at[lax.rem(j, 2), pl.ds(2 * half, 2), j // 2]

        def single(j):
            return partial.at[lax.rem(j, 2), j // 2] if first == "x" else partial.at[j]

        self.one = TwoWaySum(Line(place, first), whole, (near, out, ends), sems.at[0])
        self.two = RingSum(Line(place, "y" if first == "x" else "x"), single, ends2, sems.at[1])

    def start(self):
        self.one.start()

    def middle(self):
        self.one.middle()

    def late(self):
        def take(half, value):
            if self.first == "x":
                self.partial[half] = value
            else:
                self.partial[2 * half : 2 * half + 2] = value

        self.one.finish(take)
        self.two.start()

    def finish(self):
        self.own[...] = self.two.finish()


def plane_scratch(first, rows, width):
    half = (2, rows, width)
    whole = (2, 2, rows, width) if first == "x" else (4, rows, width)
    shapes = ((2, *half), (2, *half), (2, 2, *half), whole, (3, rows, width))
    return [pltpu.VMEM(shape, BF) for shape in shapes]


class Gather:
    def __init__(self, place, own, full, sems):
        p = self.place = place

        def rows(z, lo=0, n=ROWS):
            return full.at[pl.ds(pl.multiple_of((p.core * 4 + lax.rem(z, 4)) * ROWS + lo, HALF), n)]

        here, left, right = rows(p.z), rows(p.z + 3), rows(p.z + 1)
        far_lo, far_hi = rows(p.z + 2, 0, HALF), rows(p.z + 2, HALF, HALF)
        left_lo, right_hi = rows(p.z + 3, 0, HALF), rows(p.z + 1, HALF, HALF)
        sib = p.sibling()
        self.keep = pltpu.make_async_copy(own, here, sems.at[0, 9])
        self.c = [
            remote(own, here, sems, 0, p.right()),
            remote(own, here, sems, 1, p.left()),
            remote(own, here, sems, 2, sib),
            remote(left_lo, left_lo, sems, 3, p.right()),
            remote(right_hi, right_hi, sems, 4, p.left()),
            remote(left, left, sems, 5, sib),
            remote(right, right, sems, 6, sib),
            remote(far_lo, far_lo, sems, 7, sib),
            remote(far_hi, far_hi, sems, 8, sib),
        ]

    def start(self):
        self.keep.start()
        for i in (0, 1, 2):
            self.c[i].start()

    def middle(self):
        self.c[0].wait_recv()
        self.c[3].start()
        self.c[1].wait_recv()
        self.c[4].start()
        self.c[5].start()
        self.c[6].start()

    def late(self):
        self.c[3].wait_recv()
        self.c[7].start()
        self.c[4].wait_recv()
        self.c[8].start()

    def finish(self):
        self.keep.wait()
        for i in (0, 1, 3, 4):
            self.c[i].wait_send()
        for i in (2, 5, 6, 7, 8):
            self.c[i].wait()

    def hand_on(self):
        self.middle()
        self.late()


class Scatter:
    def __init__(self, place, terms, scratch, sems):
        p = self.place = place
        self.here, self.there, self.out, self.near, self.ends = scratch
        z = p.z
        self.order = [lax.rem(z + 2, 4), lax.rem(z + 1, 4), lax.rem(z + 3, 4), z]

        def rows(core, zz):
            return terms.at[pl.ds(pl.multiple_of((core * 4 + zz) * ROWS, ROWS), ROWS)]

        sib, right, left = p.sibling(), p.right(), p.left()
        self.cross, self.load = [], []
        for n, zz in enumerate(self.order):
            self.cross.append(remote(rows(1 - p.core, zz), self.there.at[n], sems, n, sib))
            self.load.append(pltpu.make_async_copy(rows(p.core, zz), self.here.at[n], sems.at[0, 10 + n]))
        lo, hi = pl.ds(0, HALF), pl.ds(HALF, HALF)
        out, near, ends = self.out, self.near, self.ends
        self.far_lo = remote(out.at[0, lo], near.at[0], sems, 4, right)
        self.far_hi = remote(out.at[0, hi], near.at[1], sems, 5, left)
        self.right_hi = remote(out.at[1, hi], ends.at[0, hi], sems, 6, right)
        self.left_lo = remote(out.at[2, lo], ends.at[1, lo], sems, 7, left)
        self.right_lo = remote(out.at[1, lo], ends.at[0, lo], sems, 8, right)
        self.left_hi = remote(out.at[2, hi], ends.at[1, hi], sems, 9, left)

    def start(self):
        for a, b in zip(self.cross, self.load):
            a.start()
            b.start()

    def pair(self, n, rows=slice(None)):
        return self.here[n, rows].astype(F32) + self.there[n, rows].astype(F32)

    def arrived(self, n):
        self.load[n].wait()
        self.cross[n].wait()

    def middle(self):
        self.arrived(0)
        self.out[0] = self.pair(0).astype(BF)
        self.far_lo.start()
        self.far_hi.start()
        lo, hi = slice(0, HALF), slice(HALF, ROWS)
        self.arrived(1)
        self.out[1, hi] = self.pair(1, hi).astype(BF)
        self.right_hi.start()
        self.arrived(2)
        self.out[2, lo] = self.pair(2, lo).astype(BF)
        self.left_lo.start()
        self.arrived(3)

    def late(self):
        lo, hi = slice(0, HALF), slice(HALF, ROWS)
        self.far_lo.wait_recv()
        self.out[1, lo] = (self.pair(1, lo) + self.near[0].astype(F32)).astype(BF)
        self.right_lo.start()
        self.far_hi.wait_recv()
        self.out[2, hi] = (self.pair(2, hi) + self.near[1].astype(F32)).astype(BF)
        self.left_hi.start()

    def finish(self):
        for c in (self.right_hi, self.left_lo, self.right_lo, self.left_hi):
            c.wait()
        self.far_lo.wait_send()
        self.far_hi.wait_send()
        return self.pair(3) + self.ends[0].astype(F32) + self.ends[1].astype(F32)


def scatter_scratch(d):
    return [
        pltpu.VMEM((4, ROWS, d), BF),
        pltpu.VMEM((4, ROWS, d), BF),
        pltpu.VMEM((3, ROWS, d), BF),
        pltpu.VMEM((2, HALF, d), BF),
        pltpu.VMEM((2, ROWS, d), BF),
    ]


GATHER_SEMS = pltpu.SemaphoreType.DMA((2, 10))
SCATTER_SEMS = pltpu.SemaphoreType.DMA((2, 14))
PLANE_SEMS = pltpu.SemaphoreType.DMA((2, 16))
RING_SEMS = pltpu.SemaphoreType.DMA((2, 2, 6))


def peers_of(place):
    return [
        place.at(yhi=lax.rem(place.yhi + i, 2), z=lax.rem(place.z + j, 4)) for i in range(2) for j in range(4) if i or j
    ]


def normed(x, gain):
    return x * lax.rsqrt(jnp.mean(x * x, -1, keepdims=True) + EPS) * gain


def norm_back(x, gain, grad):
    r = lax.rsqrt(jnp.mean(x * x, -1, keepdims=True) + EPS)
    weighted = gain * grad
    by_x = r * weighted - x * (r * r * r) * jnp.mean(x * weighted, -1, keepdims=True)
    return by_x, jnp.sum(grad * x * r, 0, keepdims=True)


def entry_kernel(x_ref, gain_ref, head_ref, wa_ref, wb_ref, ra_ref, rb_ref, g_ref, xs_ref, heads_ref, fulla_ref, fullb_ref,
                 ras_ref, rbs_ref, gs_ref, rows_ref, own, wa, wb, sw_sems, a_sems, b_sems, ga_sems):
    place = Place()
    greet(place, ("x", "y", "z"), True)
    pairs = ((x_ref, xs_ref), (wb_ref, wb), (wa_ref, wa), (head_ref, heads_ref), (ra_ref, ras_ref), (rb_ref, rbs_ref), (g_ref, gs_ref))
    swaps = [Swap(place, a, b, sw_sems, i) for i, (a, b) in enumerate(pairs)]
    for swap in swaps[:4]:
        swap.start()
    first = PlaneGather(place, "x", wa, fulla_ref, a_sems)
    second = PlaneGather(place, "y", wb, fullb_ref, b_sems)
    ring = Gather(place, own, rows_ref, ga_sems)
    swaps[0].wait()
    own[...] = normed(xs_ref[...].astype(F32), gain_ref[...]).astype(BF)
    ring.start()
    swaps[1].wait()
    second.start()
    swaps[2].wait()
    first.start()
    swaps[4].start()
    swaps[5].start()
    second.middle()
    first.middle()
    swaps[6].start()
    ring.middle()
    ring.late()
    second.late()
    first.late()
    ring.finish()
    second.finish()
    first.finish()
    for swap in swaps[3:]:
        swap.wait()


def sum_norm_gather_kernel(terms_ref, x_ref, gain_ref, stream_ref, rows_ref, own, here, there, out, near, ends, sc_sems, ga_sems):
    place = Place()
    greet(place, ("z",))
    terms = Scatter(place, terms_ref, (here, there, out, near, ends), sc_sems)
    terms.start()
    terms.middle()
    terms.late()
    stream = x_ref[...].astype(F32) + terms.finish()
    own[...] = normed(stream, gain_ref[...]).astype(BF)
    ring = Gather(place, own, rows_ref, ga_sems)
    ring.start()
    stream_ref[...] = stream
    ring.hand_on()
    ring.finish()


def sum_back_gather_kernel(terms_ref, stream_ref, gain_ref, g_ref, grad_ref, dgain_ref, rows_ref, own, here, there, out,
                           near, ends, sc_sems, ga_sems):
    place = Place()
    greet(place, ("z",))
    terms = Scatter(place, terms_ref, (here, there, out, near, ends), sc_sems)
    terms.start()
    terms.middle()
    terms.late()
    grad = terms.finish()
    by_x, by_gain = norm_back(stream_ref[...], gain_ref[...], grad)
    grad = g_ref[...].astype(F32) + by_x
    grad_ref[...] = grad
    own[...] = grad.astype(BF)
    ring = Gather(place, own, rows_ref, ga_sems)
    ring.start()
    dgain_ref[...] = by_gain
    ring.hand_on()
    ring.finish()


def exit_kernel(terms_ref, x_ref, gain_ref, grad_ref, output_ref, da_ref, db_ref, ra_ref, rb_ref, small_ref,
                final_ref, input_ref, owna_ref, ownb_ref, fra_ref, frb_ref, sums_ref, own, here, there, out, near, ends,
                a0, a1, a2, a3, a4, b0, b1, b2, b3, b4, suma, sumb,
                mine, plane_sums, total, peer_sums, sc_sems, sw_sems, a_sems, b_sems, sm_sems, pe_sems):
    place = Place()
    greet(place, ("x", "y", "z"), False, True, True)
    d = gain_ref.shape[1]
    pairs = (
        (output_ref, final_ref), (ra_ref, fra_ref), (rb_ref, frb_ref), (suma, owna_ref), (sumb, ownb_ref), (own, input_ref),
    )
    swaps = [Swap(place, a, b, sw_sems, i) for i, (a, b) in enumerate(pairs)]
    first = PlaneSum(place, "y", da_ref, (a0, a1, a2, a3, a4), suma, a_sems)
    second = PlaneSum(place, "x", db_ref, (b0, b1, b2, b3, b4), sumb, b_sems)
    ring = Scatter(place, terms_ref, (here, there, out, near, ends), sc_sems)
    ring.start()
    first.start()
    second.start()
    swaps[0].start()
    swaps[1].start()
    swaps[2].start()
    ring.middle()
    first.middle()
    second.middle()
    ring.late()
    first.late()
    second.late()
    grad = ring.finish()
    by_x, by_gain = norm_back(x_ref[...].astype(F32), gain_ref[...], grad)
    own[...] = (grad_ref[...] + by_x).astype(BF)
    swaps[5].start()
    mine[...] = small_ref[...]
    for i in range(d // 128):
        mine[i : i + 1, :] = by_gain[:, i * 128 : (i + 1) * 128]
    small = PlaneSame(place, mine, plane_sums, sm_sems)
    small.start()
    first.finish()
    swaps[3].start()
    second.finish()
    swaps[4].start()
    small.wait()
    subtotal = plane_sums[0]
    for i in range(1, 16):
        subtotal = subtotal + plane_sums[i]
    total[...] = subtotal
    n = peer_sums.shape[1]
    copies = [
        remote(total.at[pl.ds(0, n)], peer_sums.at[i], pe_sems, i, device) for i, device in enumerate(peers_of(place))
    ]
    for copy in copies:
        copy.start()
    sums_ref[...] = subtotal
    for copy in copies:
        copy.wait()
    gains = subtotal[:n]
    for i in range(7):
        gains = gains + peer_sums[i]
    sums_ref[0:n, :] = gains
    for swap in swaps:
        swap.wait()


class PlaneSame(Plane):
    def __init__(self, place, src, dst, sems):
        Plane.__init__(self, place, False, Same(src), dst, sems)


class Same:
    def __init__(self, ref):
        self.ref = ref
        self.at = self

    def __getitem__(self, index):
        return self.ref


HI = lax.Precision.HIGHEST
LO = lax.Precision.DEFAULT
NN = (((1,), (0,)), ((), ()))
NT = (((1,), (1,)), ((), ()))
TN = (((0,), (0,)), ((), ()))


X3 = "three"


def mm(a, b, dims=NN, precision=HI):
    if precision == X3:
        a_hi, b_hi = a.astype(jnp.bfloat16), b.astype(jnp.bfloat16)
        a_lo = (a - a_hi.astype(F32)).astype(jnp.bfloat16)
        b_lo = (b - b_hi.astype(F32)).astype(jnp.bfloat16)
        one = functools.partial(lax.dot_general, dimension_numbers=dims, preferred_element_type=F32)
        return one(a_hi, b_hi) + (one(a_hi, b_lo) + one(a_lo, b_hi))
    return lax.dot_general(a, b, dims, precision=precision, preferred_element_type=F32)


def chunk_masks():
    row = lax.broadcasted_iota(jnp.int32, (C, C), 0)
    col = lax.broadcasted_iota(jnp.int32, (C, C), 1)
    return row, col


def decay_parts(g, row, col):
    lower = (row >= col).astype(F32)
    cum = mm(lower, g)
    table = jnp.where(row >= col, jnp.exp(jnp.where(row >= col, cum - cum.T, 0.0)), 0.0)
    last = cum[C - 1 : C, :]
    return table, jnp.exp(cum), jnp.exp(last - cum), jnp.exp(last)


def wide(x):
    return jnp.concatenate([x, x], axis=1)


def inverse_many(systems, row, col, prec):
    eye = (row == col).astype(F32)
    near = (row // 8) == (col // 8)
    a1 = [jnp.where(near, a, 0.0) for a in systems]
    a2 = [mm(a, a, precision=prec) for a in a1]
    x = [eye - a for a in a1]
    a4 = [mm(a, a, precision=prec) for a in a2]
    x = [y + mm(y, a, precision=prec) for y, a in zip(x, a2)]
    x = [y + mm(y, a, precision=prec) for y, a in zip(x, a4)]
    size = 8
    while size < C:
        pick = ((row // (2 * size)) == (col // (2 * size))) & ((row // size) != (col // size))
        off = [jnp.where(pick, a, 0.0) for a in systems]
        y = [mm(o, t, precision=prec) for o, t in zip(off, x)]
        x = [t - mm(t, z, precision=prec) for t, z in zip(x, y)]
        size *= 2
    return x


def fwd_kernel(P_, group, q_ref, k_ref, v_ref, b_ref, g_ref, grow_ref, wa_ref, wb_ref, o_ref, t_ref, u_ref, s_ref, f_ref, w_ref,
               grows_ref, fulla_ref, fullb_ref, z_ref, a_sems, b_sems, ga_sems):
    place = Place()
    greet(place, ("x", "y", "z"))
    first = PlaneGather(place, "x", wa_ref, fulla_ref, a_sems)
    second = PlaneGather(place, "y", wb_ref, fullb_ref, b_sems)
    ring = Gather(place, grow_ref, grows_ref, ga_sems)
    second.start()
    first.start()
    ring.start()
    nb = q_ref.shape[0] // C
    row, col = chunk_masks()

    def parts(i, _):
        cs = [pl.ds(pl.multiple_of((i * group + j) * C, C), C) for j in range(group)]
        q = [q_ref[c, :] for c in cs]
        k = [k_ref[c, :] for c in cs]
        v = [v_ref[c, :] for c in cs]
        b = [b_ref[c, :] for c in cs]
        parts = [decay_parts(g_ref[c, :], row, col) for c in cs]
        kk = [mm(x, x, NT, P_["kk"]) for x in k]
        system = [jnp.where(row > col, bb * x * p[0], 0.0) for bb, x, p in zip(b, kk, parts)]
        t = inverse_many(system, row, col, P_["inv"])
        w = [mm(tt, bb * p[1] * x, precision=P_["w"]) for tt, bb, p, x in zip(t, b, parts, k)]
        u0 = [mm(tt, wide(bb) * x, precision=P_["u"]) for tt, bb, x in zip(t, b, v)]
        kd = [x * p[2] for x, p in zip(k, parts)]
        eye = (row == col).astype(F32)
        for c, kdd, ww, uu, tt, p in zip(cs, kd, w, u0, t, parts):
            t_ref[c, :] = tt
            w_ref[c, :] = ww
            u_ref[c, :] = uu
            f_ref[c, :] = eye * p[3] - mm(kdd, ww, TN, P_["f"])
            z_ref[c, :] = mm(kdd, uu, TN, P_["z"])
        return 0

    parts(0, 0)
    second.middle()
    first.middle()
    parts(1, 0)
    state = jnp.zeros((C, v_ref.shape[1]), F32)
    for i in range(nb):
        c = pl.ds(i * C, C)
        s_ref[c, :] = state
        if i < nb - 1:
            state = z_ref[c, :] + mm(f_ref[c, :], state, precision=P_["chain"])
    ring.middle()

    def last(i, _):
        cs = [pl.ds(pl.multiple_of((i * group + j) * C, C), C) for j in range(group)]
        for c in cs:
            q, k, s = q_ref[c, :], k_ref[c, :], s_ref[c, :]
            table, scale, _, _ = decay_parts(g_ref[c, :], row, col)
            u = u_ref[c, :] - mm(w_ref[c, :], s, precision=P_["ws"])
            u_ref[c, :] = u
            scores = mm(q, k, NT, P_["qk"]) * table
            o_ref[c, :] = mm(q * scale, s, precision=P_["o"]) + mm(scores, u, precision=P_["o"])
        return 0

    lax.fori_loop(0, nb // group, last, 0)
    second.late()
    first.late()
    ring.late()
    ring.finish()
    second.finish()
    first.finish()


def bwd_kernel(P_, group, q_ref, k_ref, v_ref, b_ref, g_ref, t_ref, u_ref, s_ref, f_ref, w_ref, do_ref,
               terms_ref, stream_ref, da_ref, db2_ref, dq_ref, dk_ref, dv_ref, db_ref, dg_ref, output_ref, owna_ref, ownb_ref,
               ds_ref, x_ref, here, there, out, near, ends,
               a0, a1, a2, a3, a4, b0, b1, b2, b3, b4, sc_sems, a_sems, b_sems):
    place = Place()
    greet(place, ("x", "y", "z"))
    sum_a = PlaneSum(place, "y", da_ref, (a0, a1, a2, a3, a4), owna_ref, a_sems)
    sum_b = PlaneSum(place, "x", db2_ref, (b0, b1, b2, b3, b4), ownb_ref, b_sems)
    ring = Scatter(place, terms_ref, (here, there, out, near, ends), sc_sems)
    ring.start()
    sum_a.start()
    sum_b.start()
    nb = q_ref.shape[0] // C
    row, col = chunk_masks()

    def first(i, _):
        cs = [pl.ds(pl.multiple_of((i * group + j) * C, C), C) for j in range(group)]
        for c in cs:
            q, k, do = q_ref[c, :], k_ref[c, :], do_ref[c, :]
            table, scale, _, _ = decay_parts(g_ref[c, :], row, col)
            scores = mm(q, k, NT, P_["qk"]) * table
            x = mm(scores, do, TN, P_["bx"])
            x_ref[c, :] = x
            ds_ref[c, :] = mm(q * scale, do, TN, P_["bx"]) - mm(w_ref[c, :], x, TN, P_["bx"])
        return 0

    lax.fori_loop(0, nb // group, first, 0)
    ring.middle()
    sum_a.middle()
    sum_b.middle()
    carry = jnp.zeros((C, v_ref.shape[1]), F32)
    for i in reversed(range(nb)):
        c = pl.ds(i * C, C)
        own = ds_ref[c, :]
        ds_ref[c, :] = carry
        if i > 0:
            carry = own + mm(f_ref[c, :], carry, TN, P_["chain"])
    def last(i, _):
        cs = [pl.ds(pl.multiple_of((i * group + j) * C, C), C) for j in range(group)]
        for c in cs:
            q, k, v, b, do = q_ref[c, :], k_ref[c, :], v_ref[c, :], b_ref[c, :], do_ref[c, :]
            t, u, s, ds = t_ref[c, :], u_ref[c, :], s_ref[c, :], ds_ref[c, :]
            table, scale, tail, total = decay_parts(g_ref[c, :], row, col)
            p = P_["bl"]
            qk = mm(q, k, NT, p)
            kk = mm(k, k, NT, p)
            ks = mm(k, s, precision=p)
            qs = mm(q, s, precision=p)
            kd = k * tail
            du = x_ref[c, :] + mm(kd, ds, precision=p)
            dr = mm(t, du, TN, P_["bt"])
            dp = jnp.where(row >= col, mm(do, u, NT, p), 0.0)
            da = jnp.where(row > col, -mm(dr, u, NT, p), 0.0)
            dqk = dp * table
            dkk = da * b * table
            n = dqk * qk + dkk * kk
            dkd = mm(u, ds, NT, p)
            dq_ref[c, :] = scale * mm(do, s, NT, p) + mm(dqk, k, precision=p)
            bdr = wide(b) * dr
            dk_ref[c, :] = (
                mm(dqk, q, TN, p)
                + mm(dkk, k, precision=p)
                + mm(dkk, k, TN, p)
                + dkd * tail
                - scale * mm(bdr, s, NT, p)
            )
            dv_ref[c, :] = bdr
            sc2 = wide(scale)
            db = jnp.sum(dr * (v - sc2 * ks), 1, keepdims=True) + jnp.sum(da * table * kk, 1, keepdims=True)
            db_ref[c, :] = jnp.broadcast_to(db, (C, C))
            tails = jnp.sum(dkd * kd, 1, keepdims=True)
            dcum = (
                jnp.sum(n, 1, keepdims=True)
                - jnp.sum(n.T, 1, keepdims=True)
                + jnp.sum(sc2 * (do * qs - bdr * ks), 1, keepdims=True)
                - tails
            )
            dcum = jnp.broadcast_to(dcum, (C, C))
            extra = jnp.sum(tails) + jnp.sum(ds * s * wide(jnp.broadcast_to(total, (C, C))))
            upper = (row <= col).astype(F32)
            dg_ref[c, :] = mm(upper, dcum) + extra
        return 0

    half = nb // group // 2
    ring.late()
    lax.fori_loop(0, half, last, 0)
    sum_a.late()
    sum_b.late()
    lax.fori_loop(half, nb // group, last, 0)
    output_ref[...] = (stream_ref[...] + ring.finish()).astype(BF)
    sum_a.finish()
    sum_b.finish()


KEYS = ("kk", "inv", "w", "u", "f", "z", "chain", "ws", "qk", "o", "bx", "bl", "bt")
PRECS = {key: X3 for key in KEYS}
VM = pl.BlockSpec(memory_space=pltpu.VMEM)
ANY = pl.BlockSpec(memory_space=pl.ANY)


def call(kernel, name, number, ins, in_specs, outs, out_specs, scratch):
    return pl.pallas_call(
        kernel,
        name=name,
        out_shape=[jax.ShapeDtypeStruct(s, t) for s, t in outs],
        in_specs=in_specs,
        out_specs=out_specs,
        scratch_shapes=scratch,
        compiler_params=pltpu.CompilerParams(
            collective_id=number, has_side_effects=True, vmem_limit_bytes=48 * 2**20
        ),
    )(*ins)


def causal_conv(inputs, taps):
    length = inputs.shape[0]
    padded = jnp.pad(inputs, ((taps.shape[0] - 1, 0), (0, 0)))
    summed = padded[0:length] * taps[0]
    for shift_at in range(1, taps.shape[0]):
        summed = summed + padded[shift_at : shift_at + length] * taps[shift_at]
    return summed


def before_delta(qk_pre, v_pre, bd_pre, conv_qk, conv_v, decay_log, decay_bias):
    dk = qk_pre.shape[-1] // 2
    rows = jax.nn.silu(causal_conv(qk_pre, conv_qk))
    q, k = rows[:, :dk], rows[:, dk:]
    q = q * lax.rsqrt(jnp.sum(q * q, -1, keepdims=True) + EPS) * dk ** (-0.5)
    k = k * lax.rsqrt(jnp.sum(k * k, -1, keepdims=True) + EPS)
    v = jax.nn.silu(causal_conv(v_pre, conv_v))
    b = jax.nn.sigmoid(bd_pre[:, 0])
    g = -jnp.exp(decay_log) * jax.nn.softplus(bd_pre[:, 1] + decay_bias)
    return q, k, v, jnp.broadcast_to(b[:, None], (b.shape[0], C)), jnp.broadcast_to(g[:, None], (g.shape[0], C))


def after_delta(delta_out, gates, gain):
    r = lax.rsqrt(jnp.mean(delta_out * delta_out, -1, keepdims=True) + GATED_EPS)
    return delta_out * r * gain * jax.nn.silu(gates)


def dot(a, b, dims=NN):
    return lax.dot_general(a, b, dims, preferred_element_type=F32)


def padded(x, width):
    return jnp.pad(x, ((0, 0), (0, width - x.shape[1])))


def up_to(n, k):
    return -(-n // k) * k


def body(
    block_input,
    mixer_gain,
    query_key_weight,
    value_gate_weight,
    beta_decay_weight,
    conv_query_key,
    conv_value,
    decay_log,
    decay_bias,
    out_gain,
    out_weight,
    forward_gain,
    gate_up_weight,
    down_weight,
    out_cotangent,
):
    d = block_input.shape[2]
    n = block_input.shape[1] * 8
    nqk, nvg, nbd = query_key_weight.shape[-1], value_gate_weight.shape[-1], beta_decay_weight.shape[-1]
    ff = gate_up_weight.shape[-1]
    dv = out_weight.shape[2]
    own_d = query_key_weight.shape[1]
    wide_a = up_to(nqk + nbd, 128)
    first_a = padded(jnp.concatenate([query_key_weight[0, :, 0], beta_decay_weight[0, :, 0]], 1), wide_a)
    first_b = value_gate_weight[0, :, 0]
    rest_a = gate_up_weight[0].reshape(-1, 2 * ff)
    rest_b = jnp.concatenate([out_weight[0, 0].T, down_weight[0].T], 1)
    taps = conv_query_key.shape[1]
    heads = jnp.concatenate(
        [
            conv_query_key[0, :, 0].reshape(-1, 128),
            conv_value[0, :, 0].reshape(-1, 128),
            padded(jnp.concatenate([decay_log, decay_bias], 1), 128),
        ]
    )
    head_rows = up_to(heads.shape[0], 8)
    heads = jnp.pad(heads, ((0, head_rows - heads.shape[0]), (0, 0)))
    sems = pltpu.SemaphoreType.DMA
    block = (ROWS, d)

    shard = lambda w: ((own_d, w), BF)
    plane = lambda w: ((2, 4, 2, own_d, w), BF)
    scratch = lambda w: pltpu.VMEM((own_d, w), BF)
    x, heads, w_a, w_b, rest_a, rest_b, g, rows = call(
        entry_kernel,
        "entry_exchange",
        0,
        (block_input[0], mixer_gain, heads, first_a, first_b, rest_a, rest_b, out_cotangent[0]),
        [VM, VM, VM, VM, VM, ANY, ANY, ANY],
        [(block, BF), (heads.shape, F32), plane(wide_a), plane(nvg), shard(2 * ff), shard(dv + ff), (block, BF), ((n, d), BF)],
        [VM, VM] + [ANY] * 6,
        [pltpu.VMEM(block, BF), scratch(wide_a), scratch(nvg), sems((2, 7)), RING_SEMS, RING_SEMS, GATHER_SEMS],
    )
    w_a, w_b = w_a.reshape(d, wide_a), w_b.reshape(d, nvg)
    size = taps * nqk // 128
    conv_qk, conv_v = heads[:size].reshape(taps, nqk), heads[size : 2 * size].reshape(taps, dv)
    decays = heads[2 * size]

    pre_a, pre_b = dot(rows, w_a), dot(rows, w_b)
    gates = pre_b[:, dv:]
    (q, k, v, b, ld), pre_back = jax.vjp(
        before_delta, pre_a[:, :nqk], pre_b[:, :dv], pre_a[:, nqk : nqk + nbd], conv_qk, conv_v, decays[0], decays[1]
    )
    f = lambda width: ((n, width), F32)
    delta_out, t, u, s, fm, w, g_rows, w_gu, w_od = call(
        functools.partial(fwd_kernel, PRECS, 4),
        "delta_forward",
        1,
        (q, k, v, b, ld, g, rest_a, rest_b),
        [VM] * 5 + [ANY] * 3,
        [f(dv), f(C), f(dv), f(dv), f(C), f(C), ((n, d), BF), plane(2 * ff), plane(dv + ff)],
        [VM] * 6 + [ANY] * 3,
        [pltpu.VMEM((n, dv), F32), RING_SEMS, RING_SEMS, GATHER_SEMS],
    )
    w_gu, w_od = w_gu.reshape(d, 2 * ff), w_od.reshape(d, dv + ff)
    w_out, w_down = w_od[:, :dv], w_od[:, dv:]
    mixed, post_back = jax.vjp(after_delta, delta_out, gates, out_gain)
    mixed = mixed.astype(BF)
    stream, forward_rows = call(
        sum_norm_gather_kernel,
        "sum_norm_gather",
        2,
        (dot(mixed, w_out, NT).astype(BF), x, forward_gain),
        [ANY, VM, VM],
        [(block, F32), ((n, d), BF)],
        [VM, ANY],
        [pltpu.VMEM(block, BF)] + scatter_scratch(d) + [SCATTER_SEMS, GATHER_SEMS],
    )
    gate = dot(forward_rows, w_gu[:, :ff])
    up = dot(forward_rows, w_gu[:, ff:])
    sg = jax.nn.sigmoid(gate)
    hidden = (gate * sg * up).astype(BF)
    grad_hidden = dot(g_rows, w_down)
    grad_gu = jnp.concatenate(
        [(grad_hidden * up * sg * (1.0 + gate * (1.0 - sg))).astype(BF), (grad_hidden * gate * sg).astype(BF)], 1
    )
    grad_stream, grad_fgain, m_rows = call(
        sum_back_gather_kernel,
        "sum_back_gather",
        3,
        (dot(grad_gu, w_gu, NT).astype(BF), stream, forward_gain, g),
        [ANY, VM, VM, VM],
        [(block, F32), ((1, d), F32), ((n, d), BF)],
        [VM, VM, ANY],
        [pltpu.VMEM(block, BF)] + scatter_scratch(d) + [SCATTER_SEMS, GATHER_SEMS],
    )
    grads_a = dot(forward_rows, grad_gu, TN).astype(BF).reshape(2, 4, 2, own_d, 2 * ff)
    grads_b = jnp.concatenate([dot(m_rows, mixed, TN).astype(BF), dot(g_rows, hidden, TN).astype(BF)], 1)
    grads_b = grads_b.reshape(2, 4, 2, own_d, dv + ff)
    grad_delta, grad_gates, grad_ogain = post_back(dot(m_rows, w_out))
    dq, dk, dvalue, db, dg, output, own_a, own_b = call(
        functools.partial(bwd_kernel, PRECS, 2),
        "delta_backward",
        4,
        (q, k, v, b, ld, t, u, s, fm, w, grad_delta, dot(hidden, w_down, NT).astype(BF), stream, grads_a, grads_b),
        [VM] * 11 + [ANY, VM, VM, VM],
        [f(C), f(C), f(dv), f(C), f(C), (block, BF), shard(2 * ff), shard(dv + ff)],
        [VM] * 8,
        [pltpu.VMEM((n, dv), F32)] * 2 + scatter_scratch(d)
        + plane_scratch("y", own_d, 2 * ff) + plane_scratch("x", own_d, dv + ff)
        + [SCATTER_SEMS, RING_SEMS, RING_SEMS],
    )
    share = 1.0 / C
    d_qk, d_v, d_bd, grad_cqk, grad_cv, grad_dlog, grad_dbias = pre_back((dq, dk, dvalue, db * share, dg * share))
    d_a = padded(jnp.concatenate([d_qk, d_bd], 1).astype(BF), wide_a)
    d_b = jnp.concatenate([d_v, grad_gates], 1).astype(BF)
    gain_rows = up_to((2 * d + dv) // 128, 8)
    zero = jnp.zeros((1, 128), F32)
    small = jnp.concatenate(
        [
            jnp.zeros((d // 128, 128), F32),
            grad_fgain.reshape(-1, 128),
            grad_ogain.reshape(-1, 128),
            jnp.zeros((gain_rows - (2 * d + dv) // 128, 128), F32),
            grad_cqk.reshape(-1, 128),
            grad_cv.reshape(-1, 128),
            padded(jnp.stack([grad_dlog, grad_dbias])[None], 128),
            jnp.zeros((head_rows - 2 * size - 1, 128), F32),
        ]
    )
    small_rows = small.shape[0]
    final, input_grad, in_a, in_b, rest_a, rest_b, sums = call(
        exit_kernel,
        "exit_exchange",
        5,
        (
            (dot(d_a, w_a, NT) + dot(d_b, w_b, NT)).astype(BF),
            x,
            mixer_gain,
            grad_stream,
            output,
            dot(rows, d_a, TN).astype(BF).reshape(2, 4, 2, own_d, wide_a),
            dot(rows, d_b, TN).astype(BF).reshape(2, 4, 2, own_d, nvg),
            own_a,
            own_b,
            small,
        ),
        [ANY, VM, VM, VM, VM, VM, VM, VM, VM, VM],
        [(block, BF), (block, BF), shard(wide_a), shard(nvg), shard(2 * ff), shard(dv + ff), ((small_rows, 128), F32)],
        [ANY] * 6 + [VM],
        [pltpu.VMEM(block, BF)]
        + scatter_scratch(d)
        + plane_scratch("y", own_d, wide_a) + plane_scratch("x", own_d, nvg)
        + [scratch(wide_a), scratch(nvg)]
        + [
            pltpu.VMEM((small_rows, 128), F32),
            pltpu.VMEM((16, small_rows, 128), F32),
            pltpu.VMEM((small_rows, 128), F32),
            pltpu.VMEM((7, gain_rows, 128), F32),
            SCATTER_SEMS,
            sems((2, 6)),
            RING_SEMS,
            RING_SEMS,
            PLANE_SEMS,
            sems((2, 7)),
        ],
    )
    in_a, in_b, rest_a, rest_b = (a.astype(F32) for a in (in_a, in_b, rest_a, rest_b))
    k8 = d // 128
    hs = sums[gain_rows:]
    return (
        final.astype(F32)[None],
        input_grad.astype(F32)[None],
        sums[:k8].reshape(1, d),
        in_a[None, :, None, :nqk],
        in_b[None, :, None],
        in_a[None, :, None, nqk : nqk + nbd],
        hs[:size].reshape(1, taps, 1, nqk),
        hs[size : 2 * size].reshape(1, taps, 1, dv),
        hs[2 * size : 2 * size + 1, :1],
        hs[2 * size : 2 * size + 1, 1:2],
        sums[2 * k8 : 2 * k8 + dv // 128].reshape(1, dv),
        rest_b[:, :dv].T[None, None],
        sums[k8 : 2 * k8].reshape(1, d),
        rest_a.reshape(1, -1, 2, ff),
        rest_b[:, dv:].T[None],
    )


def solution(mesh):
    parts = Mesh(mesh.devices.reshape(2, 4, 2, 2, 4), AXES)
    dp, tp = ("ylo", "x", "core"), ("yhi", "z")
    stream = P(dp, tp, None)
    head = P(None, tp)
    proj = P(None, dp, tp, None)
    conv = P(None, None, tp, None)
    out_w, gu_w, down_w = P(None, tp, None, dp), P(None, dp, None, tp), P(None, tp, dp)
    return jax.shard_map(
        body,
        mesh=parts,
        in_specs=(stream, P(), proj, proj, proj, conv, conv, head, head, P(), out_w, P(), gu_w, down_w, stream),
        out_specs=(stream, stream, P(), proj, proj, proj, conv, conv, head, head, P(), out_w, P(), gu_w, down_w),
        check_vma=False,
    )
```

```python
import functools

import jax
import jax.numpy as jnp
from jax import lax
from jax.experimental import pallas as pl
from jax.experimental.pallas import tpu as pltpu
from jax.sharding import Mesh
from jax.sharding import PartitionSpec as P
C = 128
F32 = jnp.float32
BF = jnp.bfloat16
EPS = 1e-06
GATED_EPS = 1e-05
AXES = ("ylo", "x", "core", "yhi", "z")
MESH_ID = pl.DeviceIdType.MESH
ROWS = 128
HALF = 64


class Place:
    def __init__(self):
        self.ylo, self.x, self.core, self.yhi, self.z = (lax.axis_index(a) for a in AXES)
        self.same = self.core == self.yhi
        self.block = self.core * 4 + self.z

    def at(self, **other):
        return {a: other.get(a, getattr(self, a)) for a in AXES}

    def sibling(self):
        return self.at(core=1 - self.core)

    def right(self):
        return self.at(z=lax.rem(self.z + 1, 4))

    def left(self):
        return self.at(z=lax.rem(self.z + 3, 4))

    def swapped(self):
        return self.at(core=self.yhi, yhi=self.core)

    def plane(self, i, j, m, flip):
        core, yhi = self.yhi, self.core
        if m and flip == "yhi":
            yhi = 1 - yhi
        if m and flip == "core":
            core = 1 - core
        return self.at(ylo=lax.rem(self.ylo + i, 2), x=lax.rem(self.x + j, 4), core=core, yhi=yhi)


OFFSETS = [(i, j, m) for i in range(2) for j in range(4) for m in range(2)]


def greet(place, lines=(), swap=False, owners=False, tensor_peers=False):
    bar = pltpu.get_barrier_semaphore()
    count = 0
    devices = [place.sibling()]
    for axis in lines:
        line = Line(place, axis)
        devices += [line.device(i) for i in ((1, 3) if axis == "z" else (1, 2, 3))]
    if tensor_peers:
        devices += peers_of(place)
    if owners:
        devices += [place.plane(i, j, m, "yhi") for i, j, m in OFFSETS[1:]]
    for device in devices:
        pl.semaphore_signal(bar, inc=1, device_id=device, device_id_type=MESH_ID)
    count = len(devices)
    if swap or owners:

        @pl.when(jnp.logical_not(place.same))
        def _():
            pl.semaphore_signal(bar, inc=1, device_id=place.swapped(), device_id_type=MESH_ID)

        count = count + jnp.where(place.same, 0, 1)
    pl.semaphore_wait(bar, count)


def remote(src, dst, sems, i, device):
    return pltpu.make_async_remote_copy(
        src_ref=src, dst_ref=dst, send_sem=sems.at[0, i], recv_sem=sems.at[1, i], device_id=device, device_id_type=MESH_ID
    )


class Swap:
    def __init__(self, place, src, dst, sems, i):
        self.place = place
        self.copy = remote(src, dst, sems, i, place.swapped())
        self.own = pltpu.make_async_copy(src, dst, sems.at[0, i])

    def start(self):
        pl.when(self.place.same)(self.own.start)
        pl.when(jnp.logical_not(self.place.same))(self.copy.start)

    def wait(self):
        pl.when(self.place.same)(self.own.wait)
        pl.when(jnp.logical_not(self.place.same))(self.copy.wait)


class Plane:
    def __init__(self, place, gather, src, dst, sems):
        self.place = place
        flip = "yhi" if gather else "core"
        mine = (place.ylo * 4 + place.x) * 2 + (place.core if gather else place.yhi)
        self.copies, self.arrivals = [], []
        for n, (i, j, m) in enumerate(OFFSETS):
            target = place.plane(i, j, m, flip)
            index = (target["ylo"] * 4 + target["x"]) * 2 + target["core"]
            part = src if gather else src.at[index]
            copy = pltpu.make_async_remote_copy(
                src_ref=part, dst_ref=dst.at[mine], send_sem=sems.at[0, n], recv_sem=sems.at[1, mine],
                device_id=target, device_id_type=MESH_ID,
            )
            other = place.yhi if gather else place.core
            slot = (lax.rem(place.ylo + i, 2) * 4 + lax.rem(place.x + j, 4)) * 2 + lax.rem(other + m, 2)
            arrival = pltpu.make_async_remote_copy(
                src_ref=part, dst_ref=dst.at[slot], send_sem=sems.at[0, n], recv_sem=sems.at[1, slot],
                device_id=target, device_id_type=MESH_ID,
            )
            self.copies.append(copy)
            self.arrivals.append(arrival)
            if n == 0:
                self.own = pltpu.make_async_copy(part, dst.at[mine], sems.at[0, 0])

    def start(self):
        pl.when(self.place.same)(self.own.start)
        pl.when(jnp.logical_not(self.place.same))(self.copies[0].start)
        for copy in self.copies[1:]:
            copy.start()

    def wait(self):
        pl.when(self.place.same)(self.own.wait)

        @pl.when(jnp.logical_not(self.place.same))
        def _():
            self.copies[0].wait_send()
            self.arrivals[0].wait_recv()

        for copy, arrival in zip(self.copies[1:], self.arrivals[1:]):
            copy.wait_send()
            arrival.wait_recv()


class Line:
    def __init__(self, place, axis):
        self.place, self.axis = place, axis
        self.me = {"x": place.x, "z": place.z, "y": place.yhi * 2 + place.ylo}[axis]

    def index(self, i):
        return lax.rem(self.me + i, 4)

    def device(self, i):
        j = self.index(i)
        if self.axis == "y":
            return self.place.at(yhi=j // 2, ylo=lax.rem(j, 2))
        return self.place.at(**{self.axis: j})


class RingGather:
    def __init__(self, line, own, part, sems):
        here = part(line.me)
        self.keep = None
        if own is None:
            own = here
        else:
            self.keep = pltpu.make_async_copy(own, here, sems.at[0, 3])
        self.c = [remote(own, here, sems, i, line.device(i + 1)) for i in (1, 0, 2)]

    def start(self):
        if self.keep is not None:
            self.keep.start()
        for c in self.c:
            c.start()

    def finish(self):
        if self.keep is not None:
            self.keep.wait()
        for c in self.c:
            c.wait()


class RingSum:
    def __init__(self, line, part, ends, sems):
        self.own, self.ends = part(line.me), ends
        self.c = [remote(part(line.index(i + 1)), ends.at[i], sems, i, line.device(i + 1)) for i in (1, 0, 2)]

    def start(self):
        for c in self.c:
            c.start()

    def finish(self):
        for c in self.c:
            c.wait()
        total = self.own[...].astype(F32)
        for i in range(3):
            total = total + self.ends[i].astype(F32)
        return total.astype(BF)


class TwoWayGather:
    def __init__(self, line, own, part, sems):
        right, left = line.device(1), line.device(3)
        here = part(line.me, None)
        self.keep = None
        if own is None:
            own = here
        else:
            self.keep = pltpu.make_async_copy(own, here, sems.at[0, 4])
        from_left, from_right = part(line.index(3), 0), part(line.index(1), 1)
        self.c = [
            remote(own, here, sems, 0, right),
            remote(own, here, sems, 1, left),
            remote(from_left, from_left, sems, 2, right),
            remote(from_right, from_right, sems, 3, left),
        ]

    def start(self):
        if self.keep is not None:
            self.keep.start()
        self.c[0].start()
        self.c[1].start()

    def middle(self):
        self.c[0].wait_recv()
        self.c[2].start()
        self.c[1].wait_recv()
        self.c[3].start()

    def finish(self):
        if self.keep is not None:
            self.keep.wait()
        self.c[0].wait_send()
        self.c[1].wait_send()
        self.c[2].wait()
        self.c[3].wait()


class TwoWaySum:
    def __init__(self, line, part, scratch, sems):
        self.line, self.part = line, part
        self.near, self.out, self.ends = near, out, ends = scratch
        right, left = line.device(1), line.device(3)
        self.c = [
            remote(part(line.index(2), 0), near.at[0], sems, 0, right),
            remote(part(line.index(2), 1), near.at[1], sems, 1, left),
            remote(part(line.index(1), 1), ends.at[0, 1], sems, 2, right),
            remote(part(line.index(3), 0), ends.at[1, 0], sems, 3, left),
            remote(out.at[0], ends.at[0, 0], sems, 4, right),
            remote(out.at[1], ends.at[1, 1], sems, 5, left),
        ]

    def start(self):
        for i in range(4):
            self.c[i].start()

    def middle(self):
        line = self.line
        for i, (j, half) in enumerate(((line.index(1), 0), (line.index(3), 1))):
            self.c[i].wait_recv()
            self.out[i] = (self.part(j, half)[...].astype(F32) + self.near[i].astype(F32)).astype(BF)
            self.c[4 + i].start()

    def finish(self, take):
        self.c[0].wait_send()
        self.c[1].wait_send()
        for i in (2, 3, 4, 5):
            self.c[i].wait()
        for half in range(2):
            own = self.part(self.line.me, half)[...].astype(F32)
            take(half, (own + self.ends[0, half].astype(F32) + self.ends[1, half].astype(F32)).astype(BF))


class PlaneGather:
    def __init__(self, place, first, own, full, sems):
        def single(j):
            if first == "x":
                return full.at[place.ylo, j, place.yhi]
            return full.at[lax.rem(j, 2), place.x, j // 2]

        def whole(j, half):
            if first == "y":
                return full.at[:, j] if half is None else full.at[half, j]
            some = slice(None) if half is None else pl.ds(2 * half, 2)
            return full.at[lax.rem(j, 2), some, j // 2]

        self.one = RingGather(Line(place, first), own, single, sems.at[0])
        self.two = TwoWayGather(Line(place, "y" if first == "x" else "x"), None, whole, sems.at[1])

    def start(self):
        self.one.start()

    def middle(self):
        self.one.finish()
        self.two.start()

    def late(self):
        self.two.middle()

    def finish(self):
        self.two.finish()


class PlaneSum:
    def __init__(self, place, first, terms, scratch, own, sems):
        near, out, ends, partial, ends2 = scratch
        self.first, self.partial, self.own = first, partial, own

        def whole(j, half):
            if first == "x":
                return terms.at[half, j]
            return terms.at[lax.rem(j, 2), pl.ds(2 * half, 2), j // 2]

        def single(j):
            return partial.at[lax.rem(j, 2), j // 2] if first == "x" else partial.at[j]

        self.one = TwoWaySum(Line(place, first), whole, (near, out, ends), sems.at[0])
        self.two = RingSum(Line(place, "y" if first == "x" else "x"), single, ends2, sems.at[1])

    def start(self):
        self.one.start()

    def middle(self):
        self.one.middle()

    def late(self):
        def take(half, value):
            if self.first == "x":
                self.partial[half] = value
            else:
                self.partial[2 * half : 2 * half + 2] = value

        self.one.finish(take)
        self.two.start()

    def finish(self):
        self.own[...] = self.two.finish()


def plane_scratch(first, rows, width):
    half = (2, rows, width)
    whole = (2, 2, rows, width) if first == "x" else (4, rows, width)
    shapes = ((2, *half), (2, *half), (2, 2, *half), whole, (3, rows, width))
    return [pltpu.VMEM(shape, BF) for shape in shapes]


class Gather:
    def __init__(self, place, own, full, sems):
        p = self.place = place

        def rows(z, lo=0, n=ROWS):
            return full.at[pl.ds(pl.multiple_of((p.core * 4 + lax.rem(z, 4)) * ROWS + lo, HALF), n)]

        here, left, right = rows(p.z), rows(p.z + 3), rows(p.z + 1)
        far_lo, far_hi = rows(p.z + 2, 0, HALF), rows(p.z + 2, HALF, HALF)
        left_lo, right_hi = rows(p.z + 3, 0, HALF), rows(p.z + 1, HALF, HALF)
        sib = p.sibling()
        self.keep = pltpu.make_async_copy(own, here, sems.at[0, 9])
        self.c = [
            remote(own, here, sems, 0, p.right()),
            remote(own, here, sems, 1, p.left()),
            remote(own, here, sems, 2, sib),
            remote(left_lo, left_lo, sems, 3, p.right()),
            remote(right_hi, right_hi, sems, 4, p.left()),
            remote(left, left, sems, 5, sib),
            remote(right, right, sems, 6, sib),
            remote(far_lo, far_lo, sems, 7, sib),
            remote(far_hi, far_hi, sems, 8, sib),
        ]

    def start(self):
        self.keep.start()
        for i in (0, 1, 2):
            self.c[i].start()

    def middle(self):
        self.c[0].wait_recv()
        self.c[3].start()
        self.c[1].wait_recv()
        self.c[4].start()
        self.c[5].start()
        self.c[6].start()

    def late(self):
        self.c[3].wait_recv()
        self.c[7].start()
        self.c[4].wait_recv()
        self.c[8].start()

    def finish(self):
        self.keep.wait()
        for i in (0, 1, 3, 4):
            self.c[i].wait_send()
        for i in (2, 5, 6, 7, 8):
            self.c[i].wait()

    def hand_on(self):
        self.middle()
        self.late()


class Scatter:
    def __init__(self, place, terms, scratch, sems):
        p = self.place = place
        self.here, self.there, self.out, self.near, self.ends = scratch
        z = p.z
        self.order = [lax.rem(z + 2, 4), lax.rem(z + 1, 4), lax.rem(z + 3, 4), z]

        def rows(core, zz):
            return terms.at[pl.ds(pl.multiple_of((core * 4 + zz) * ROWS, ROWS), ROWS)]

        sib, right, left = p.sibling(), p.right(), p.left()
        self.cross, self.load = [], []
        for n, zz in enumerate(self.order):
            self.cross.append(remote(rows(1 - p.core, zz), self.there.at[n], sems, n, sib))
            self.load.append(pltpu.make_async_copy(rows(p.core, zz), self.here.at[n], sems.at[0, 10 + n]))
        lo, hi = pl.ds(0, HALF), pl.ds(HALF, HALF)
        out, near, ends = self.out, self.near, self.ends
        self.far_lo = remote(out.at[0, lo], near.at[0], sems, 4, right)
        self.far_hi = remote(out.at[0, hi], near.at[1], sems, 5, left)
        self.right_hi = remote(out.at[1, hi], ends.at[0, hi], sems, 6, right)
        self.left_lo = remote(out.at[2, lo], ends.at[1, lo], sems, 7, left)
        self.right_lo = remote(out.at[1, lo], ends.at[0, lo], sems, 8, right)
        self.left_hi = remote(out.at[2, hi], ends.at[1, hi], sems, 9, left)

    def start(self):
        for a, b in zip(self.cross, self.load):
            a.start()
            b.start()

    def pair(self, n, rows=slice(None)):
        return self.here[n, rows].astype(F32) + self.there[n, rows].astype(F32)

    def arrived(self, n):
        self.load[n].wait()
        self.cross[n].wait()

    def middle(self):
        self.arrived(0)
        self.out[0] = self.pair(0).astype(BF)
        self.far_lo.start()
        self.far_hi.start()
        lo, hi = slice(0, HALF), slice(HALF, ROWS)
        self.arrived(1)
        self.out[1, hi] = self.pair(1, hi).astype(BF)
        self.right_hi.start()
        self.arrived(2)
        self.out[2, lo] = self.pair(2, lo).astype(BF)
        self.left_lo.start()
        self.arrived(3)

    def late(self):
        lo, hi = slice(0, HALF), slice(HALF, ROWS)
        self.far_lo.wait_recv()
        self.out[1, lo] = (self.pair(1, lo) + self.near[0].astype(F32)).astype(BF)
        self.right_lo.start()
        self.far_hi.wait_recv()
        self.out[2, hi] = (self.pair(2, hi) + self.near[1].astype(F32)).astype(BF)
        self.left_hi.start()

    def finish(self):
        for c in (self.right_hi, self.left_lo, self.right_lo, self.left_hi):
            c.wait()
        self.far_lo.wait_send()
        self.far_hi.wait_send()
        return self.pair(3) + self.ends[0].astype(F32) + self.ends[1].astype(F32)


def scatter_scratch(d):
    return [
        pltpu.VMEM((4, ROWS, d), BF),
        pltpu.VMEM((4, ROWS, d), BF),
        pltpu.VMEM((3, ROWS, d), BF),
        pltpu.VMEM((2, HALF, d), BF),
        pltpu.VMEM((2, ROWS, d), BF),
    ]


GATHER_SEMS = pltpu.SemaphoreType.DMA((2, 10))
SCATTER_SEMS = pltpu.SemaphoreType.DMA((2, 14))
PLANE_SEMS = pltpu.SemaphoreType.DMA((2, 16))
RING_SEMS = pltpu.SemaphoreType.DMA((2, 2, 6))


def peers_of(place):
    return [
        place.at(yhi=lax.rem(place.yhi + i, 2), z=lax.rem(place.z + j, 4)) for i in range(2) for j in range(4) if i or j
    ]


def normed(x, gain):
    return x * lax.rsqrt(jnp.mean(x * x, -1, keepdims=True) + EPS) * gain


def norm_back(x, gain, grad):
    r = lax.rsqrt(jnp.mean(x * x, -1, keepdims=True) + EPS)
    weighted = gain * grad
    by_x = r * weighted - x * (r * r * r) * jnp.mean(x * weighted, -1, keepdims=True)
    return by_x, jnp.sum(grad * x * r, 0, keepdims=True)


def entry_kernel(x_ref, gain_ref, head_ref, wa_ref, wb_ref, ra_ref, rb_ref, g_ref, xs_ref, heads_ref, fulla_ref, fullb_ref,
                 ras_ref, rbs_ref, gs_ref, rows_ref, own, wa, wb, sw_sems, a_sems, b_sems, ga_sems):
    place = Place()
    greet(place, ("x", "y", "z"), True)
    pairs = ((x_ref, xs_ref), (wb_ref, wb), (wa_ref, wa), (head_ref, heads_ref), (ra_ref, ras_ref), (rb_ref, rbs_ref), (g_ref, gs_ref))
    swaps = [Swap(place, a, b, sw_sems, i) for i, (a, b) in enumerate(pairs)]
    for swap in swaps[:4]:
        swap.start()
    first = PlaneGather(place, "x", wa, fulla_ref, a_sems)
    second = PlaneGather(place, "y", wb, fullb_ref, b_sems)
    ring = Gather(place, own, rows_ref, ga_sems)
    swaps[0].wait()
    own[...] = normed(xs_ref[...].astype(F32), gain_ref[...]).astype(BF)
    ring.start()
    swaps[1].wait()
    second.start()
    swaps[2].wait()
    first.start()
    swaps[4].start()
    swaps[5].start()
    second.middle()
    first.middle()
    swaps[6].start()
    ring.middle()
    ring.late()
    second.late()
    first.late()
    ring.finish()
    second.finish()
    first.finish()
    for swap in swaps[3:]:
        swap.wait()


def sum_norm_gather_kernel(terms_ref, x_ref, gain_ref, stream_ref, rows_ref, own, here, there, out, near, ends, sc_sems, ga_sems):
    place = Place()
    greet(place, ("z",))
    terms = Scatter(place, terms_ref, (here, there, out, near, ends), sc_sems)
    terms.start()
    terms.middle()
    terms.late()
    stream = x_ref[...].astype(F32) + terms.finish()
    own[...] = normed(stream, gain_ref[...]).astype(BF)
    ring = Gather(place, own, rows_ref, ga_sems)
    ring.start()
    stream_ref[...] = stream
    ring.hand_on()
    ring.finish()


def sum_back_gather_kernel(terms_ref, stream_ref, gain_ref, g_ref, grad_ref, dgain_ref, rows_ref, own, here, there, out,
                           near, ends, sc_sems, ga_sems):
    place = Place()
    greet(place, ("z",))
    terms = Scatter(place, terms_ref, (here, there, out, near, ends), sc_sems)
    terms.start()
    terms.middle()
    terms.late()
    grad = terms.finish()
    by_x, by_gain = norm_back(stream_ref[...], gain_ref[...], grad)
    grad = g_ref[...].astype(F32) + by_x
    grad_ref[...] = grad
    own[...] = grad.astype(BF)
    ring = Gather(place, own, rows_ref, ga_sems)
    ring.start()
    dgain_ref[...] = by_gain
    ring.hand_on()
    ring.finish()


def exit_kernel(terms_ref, x_ref, gain_ref, grad_ref, output_ref, da_ref, db_ref, ra_ref, rb_ref, small_ref,
                final_ref, input_ref, owna_ref, ownb_ref, fra_ref, frb_ref, sums_ref, own, here, there, out, near, ends,
                a0, a1, a2, a3, a4, b0, b1, b2, b3, b4, suma, sumb,
                mine, plane_sums, total, peer_sums, sc_sems, sw_sems, a_sems, b_sems, sm_sems, pe_sems):
    place = Place()
    greet(place, ("x", "y", "z"), False, True, True)
    d = gain_ref.shape[1]
    pairs = (
        (output_ref, final_ref), (ra_ref, fra_ref), (rb_ref, frb_ref), (suma, owna_ref), (sumb, ownb_ref), (own, input_ref),
    )
    swaps = [Swap(place, a, b, sw_sems, i) for i, (a, b) in enumerate(pairs)]
    first = PlaneSum(place, "y", da_ref, (a0, a1, a2, a3, a4), suma, a_sems)
    second = PlaneSum(place, "x", db_ref, (b0, b1, b2, b3, b4), sumb, b_sems)
    ring = Scatter(place, terms_ref, (here, there, out, near, ends), sc_sems)
    ring.start()
    first.start()
    second.start()
    swaps[0].start()
    swaps[1].start()
    swaps[2].start()
    ring.middle()
    first.middle()
    second.middle()
    ring.late()
    first.late()
    second.late()
    grad = ring.finish()
    by_x, by_gain = norm_back(x_ref[...].astype(F32), gain_ref[...], grad)
    own[...] = (grad_ref[...] + by_x).astype(BF)
    swaps[5].start()
    mine[...] = small_ref[...]
    for i in range(d // 128):
        mine[i : i + 1, :] = by_gain[:, i * 128 : (i + 1) * 128]
    small = PlaneSame(place, mine, plane_sums, sm_sems)
    small.start()
    first.finish()
    swaps[3].start()
    second.finish()
    swaps[4].start()
    small.wait()
    subtotal = plane_sums[0]
    for i in range(1, 16):
        subtotal = subtotal + plane_sums[i]
    total[...] = subtotal
    n = peer_sums.shape[1]
    copies = [
        remote(total.at[pl.ds(0, n)], peer_sums.at[i], pe_sems, i, device) for i, device in enumerate(peers_of(place))
    ]
    for copy in copies:
        copy.start()
    sums_ref[...] = subtotal
    for copy in copies:
        copy.wait()
    gains = subtotal[:n]
    for i in range(7):
        gains = gains + peer_sums[i]
    sums_ref[0:n, :] = gains
    for swap in swaps:
        swap.wait()


class PlaneSame(Plane):
    def __init__(self, place, src, dst, sems):
        Plane.__init__(self, place, False, Same(src), dst, sems)


class Same:
    def __init__(self, ref):
        self.ref = ref
        self.at = self

    def __getitem__(self, index):
        return self.ref


HI = lax.Precision.HIGHEST
LO = lax.Precision.DEFAULT
NN = (((1,), (0,)), ((), ()))
NT = (((1,), (1,)), ((), ()))
TN = (((0,), (0,)), ((), ()))


X3 = "three"


def mm(a, b, dims=NN, precision=HI):
    if precision == X3:
        a_hi, b_hi = a.astype(jnp.bfloat16), b.astype(jnp.bfloat16)
        a_lo = (a - a_hi.astype(F32)).astype(jnp.bfloat16)
        b_lo = (b - b_hi.astype(F32)).astype(jnp.bfloat16)
        one = functools.partial(lax.dot_general, dimension_numbers=dims, preferred_element_type=F32)
        return one(a_hi, b_hi) + (one(a_hi, b_lo) + one(a_lo, b_hi))
    return lax.dot_general(a, b, dims, precision=precision, preferred_element_type=F32)


def chunk_masks():
    row = lax.broadcasted_iota(jnp.int32, (C, C), 0)
    col = lax.broadcasted_iota(jnp.int32, (C, C), 1)
    return row, col


def decay_parts(g, row, col):
    lower = (row >= col).astype(F32)
    cum = mm(lower, g)
    table = jnp.where(row >= col, jnp.exp(jnp.where(row >= col, cum - cum.T, 0.0)), 0.0)
    last = cum[C - 1 : C, :]
    return table, jnp.exp(cum), jnp.exp(last - cum), jnp.exp(last)


def wide(x):
    return jnp.concatenate([x, x], axis=1)


def inverse_many(systems, row, col, prec):
    eye = (row == col).astype(F32)
    near = (row // 8) == (col // 8)
    a1 = [jnp.where(near, a, 0.0) for a in systems]
    a2 = [mm(a, a, precision=prec) for a in a1]
    x = [eye - a for a in a1]
    a4 = [mm(a, a, precision=prec) for a in a2]
    x = [y + mm(y, a, precision=prec) for y, a in zip(x, a2)]
    x = [y + mm(y, a, precision=prec) for y, a in zip(x, a4)]
    size = 8
    while size < C:
        pick = ((row // (2 * size)) == (col // (2 * size))) & ((row // size) != (col // size))
        off = [jnp.where(pick, a, 0.0) for a in systems]
        y = [mm(o, t, precision=prec) for o, t in zip(off, x)]
        x = [t - mm(t, z, precision=prec) for t, z in zip(x, y)]
        size *= 2
    return x


def rows_before(ref, i, columns):
    lead = ref[pl.ds(pl.multiple_of(jnp.maximum(i * C - 8, 0), 8), 8), columns]
    lead = jnp.where(i > 0, lead, 0.0)
    return jnp.concatenate([lead, ref[pl.ds(pl.multiple_of(i * C, C), C), columns]], 0)


def rows_after(ref, i, nb):
    tail = ref[pl.ds(pl.multiple_of(jnp.minimum((i + 1) * C, nb * C - 8), 8), 8), :]
    tail = jnp.where(i < nb - 1, tail, 0.0)
    return jnp.concatenate([ref[pl.ds(pl.multiple_of(i * C, C), C), :], tail], 0)


def conv_of(ext, taps):
    total = ext[5 : 5 + C] * taps[0:1]
    for i in range(1, 4):
        total = total + ext[5 + i : 5 + i + C] * taps[i : i + 1]
    return total


def sigmoid(x):
    return 1.0 / (1.0 + jnp.exp(-x))


def silu_slope(x, s):
    return s * (1.0 + x * (1.0 - s))


def columns(x):
    return jnp.broadcast_to(x, (C, C))


def before_delta(i, pa_ref, pb_ref, tq_ref, tv_ref, dec_ref, q_ref, k_ref, v_ref, b_ref, g_ref):
    rows = pl.ds(pl.multiple_of(i * C, C), C)
    y = conv_of(rows_before(pa_ref, i, pl.ds(0, 2 * C)), tq_ref[...])
    y = y * sigmoid(y)
    q, k = y[:, :C], y[:, C:]
    q_ref[rows, :] = q * (lax.rsqrt(jnp.sum(q * q, -1, keepdims=True) + EPS) * C ** (-0.5))
    k_ref[rows, :] = k * lax.rsqrt(jnp.sum(k * k, -1, keepdims=True) + EPS)
    y = conv_of(rows_before(pb_ref, i, pl.ds(0, 2 * C)), tv_ref[...])
    v_ref[rows, :] = y * sigmoid(y)
    bd = pa_ref[rows, pl.ds(2 * C, C)]
    b_ref[rows, :] = columns(sigmoid(bd[:, 0:1]))
    step = bd[:, 1:2] + dec_ref[0:1, 1:2]
    step = jnp.maximum(step, 0.0) + jnp.log1p(jnp.exp(-jnp.abs(step)))
    g_ref[rows, :] = columns(-jnp.exp(dec_ref[0:1, 0:1]) * step)


def after_delta(i, o_ref, pb_ref, gain_ref, mixed_ref):
    rows = pl.ds(pl.multiple_of(i * C, C), C)
    o, gates = o_ref[rows, :], pb_ref[rows, pl.ds(2 * C, 2 * C)]
    r = lax.rsqrt(jnp.mean(o * o, -1, keepdims=True) + GATED_EPS)
    mixed_ref[rows, :] = (o * r * gain_ref[...] * (gates * sigmoid(gates))).astype(BF)


def after_delta_back(i, dm_ref, o_ref, pb_ref, gain_ref, do_ref, dpb_ref, dgain_ref):
    rows = pl.ds(pl.multiple_of(i * C, C), C)
    dm, o, gates, gain = dm_ref[rows, :], o_ref[rows, :], pb_ref[rows, pl.ds(2 * C, 2 * C)], gain_ref[...]
    r = lax.rsqrt(jnp.mean(o * o, -1, keepdims=True) + GATED_EPS)
    s = sigmoid(gates)
    unit = o * r
    dpb_ref[rows, pl.ds(2 * C, 2 * C)] = (dm * unit * gain * silu_slope(gates, s)).astype(BF)
    dn = dm * (gates * s)
    dgain_ref[...] += jnp.sum(dn * unit, 0, keepdims=True)
    w = dn * gain
    do_ref[rows, :] = r * (w - unit * jnp.mean(unit * w, -1, keepdims=True))


def before_delta_back(i, pa_ref, pb_ref, tq_ref, tv_ref, dec_ref, b_ref, g_ref, dq_ref, dk_ref, dv_ref, db_ref, dg_ref,
                      cq_ref, cv_ref, dpa_ref, dtq_ref, dtv_ref, ddec_ref):
    rows = pl.ds(pl.multiple_of(i * C, C), C)
    ext = rows_before(pa_ref, i, pl.ds(0, 2 * C))
    y = conv_of(ext, tq_ref[...])
    s = sigmoid(y)
    z = y * s
    q, k, dq, dk = z[:, :C], z[:, C:], dq_ref[rows, :], dk_ref[rows, :]
    rq = lax.rsqrt(jnp.sum(q * q, -1, keepdims=True) + EPS)
    rk = lax.rsqrt(jnp.sum(k * k, -1, keepdims=True) + EPS)
    uq, uk = q * rq, k * rk
    dz_q = (rq * C ** (-0.5)) * (dq - uq * jnp.sum(uq * dq, -1, keepdims=True))
    dz_k = rk * (dk - uk * jnp.sum(uk * dk, -1, keepdims=True))
    dc = jnp.concatenate([dz_q, dz_k], 1) * silu_slope(y, s)
    cq_ref[rows, :] = dc
    for j in range(4):
        dtq_ref[j : j + 1, :] += jnp.sum(dc * ext[5 + j : 5 + j + C], 0, keepdims=True)
    ext = rows_before(pb_ref, i, pl.ds(0, 2 * C))
    y = conv_of(ext, tv_ref[...])
    s = sigmoid(y)
    dc = dv_ref[rows, :] * silu_slope(y, s)
    cv_ref[rows, :] = dc
    for j in range(4):
        dtv_ref[j : j + 1, :] += jnp.sum(dc * ext[5 + j : 5 + j + C], 0, keepdims=True)
    b = b_ref[rows, :]
    dg = dg_ref[rows, :]
    step = columns(pa_ref[rows, pl.ds(2 * C, C)][:, 1:2]) + dec_ref[0:1, 1:2]
    dstep = dg * (-jnp.exp(dec_ref[0:1, 0:1])) * sigmoid(step)
    lane = lax.broadcasted_iota(jnp.int32, (C, C), 1)
    dbd = jnp.where(lane == 0, db_ref[rows, :] * b * (1.0 - b), jnp.where(lane == 1, dstep, 0.0))
    dpa_ref[rows, pl.ds(2 * C, C)] = dbd.astype(BF)
    dlog = dg * g_ref[rows, :]
    ddec_ref[...] += jnp.sum(jnp.where(lane == 0, dlog, jnp.where(lane == 1, dstep, 0.0)), 0, keepdims=True)


def conv_back(i, nb, dc_ref, taps, out_ref):
    rows = pl.ds(pl.multiple_of(i * C, C), C)
    ext = rows_after(dc_ref, i, nb)
    total = ext[3 : 3 + C] * taps[0:1]
    for j in range(1, 4):
        total = total + ext[3 - j : 3 - j + C] * taps[j : j + 1]
    out_ref[rows, pl.ds(0, 2 * C)] = total.astype(BF)


def each_block(nb, body):
    def step(i, _):
        body(i)
        return 0

    lax.fori_loop(0, nb, step, 0)


def fwd_kernel(P_, group, pa_ref, pb_ref, tq_ref, tv_ref, dec_ref, gain_ref, grow_ref, wa_ref, wb_ref,
               mixed_ref, q_ref, k_ref, v_ref, b_ref, g_ref, o_ref, t_ref, u_ref, s_ref, f_ref, w_ref, grows_ref, fulla_ref, fullb_ref, z_ref, a_sems, b_sems, ga_sems):
    place = Place()
    greet(place, ("x", "y", "z"))
    first = PlaneGather(place, "x", wa_ref, fulla_ref, a_sems)
    second = PlaneGather(place, "y", wb_ref, fullb_ref, b_sems)
    ring = Gather(place, grow_ref, grows_ref, ga_sems)
    second.start()
    first.start()
    ring.start()
    nb = q_ref.shape[0] // C
    each_block(nb, lambda i: before_delta(i, pa_ref, pb_ref, tq_ref, tv_ref, dec_ref, q_ref, k_ref, v_ref, b_ref, g_ref))
    row, col = chunk_masks()

    def parts(i, _):
        cs = [pl.ds(pl.multiple_of((i * group + j) * C, C), C) for j in range(group)]
        q = [q_ref[c, :] for c in cs]
        k = [k_ref[c, :] for c in cs]
        v = [v_ref[c, :] for c in cs]
        b = [b_ref[c, :] for c in cs]
        parts = [decay_parts(g_ref[c, :], row, col) for c in cs]
        kk = [mm(x, x, NT, P_["kk"]) for x in k]
        system = [jnp.where(row > col, bb * x * p[0], 0.0) for bb, x, p in zip(b, kk, parts)]
        t = inverse_many(system, row, col, P_["inv"])
        w = [mm(tt, bb * p[1] * x, precision=P_["w"]) for tt, bb, p, x in zip(t, b, parts, k)]
        u0 = [mm(tt, wide(bb) * x, precision=P_["u"]) for tt, bb, x in zip(t, b, v)]
        kd = [x * p[2] for x, p in zip(k, parts)]
        eye = (row == col).astype(F32)
        for c, kdd, ww, uu, tt, p in zip(cs, kd, w, u0, t, parts):
            t_ref[c, :] = tt
            w_ref[c, :] = ww
            u_ref[c, :] = uu
            f_ref[c, :] = eye * p[3] - mm(kdd, ww, TN, P_["f"])
            z_ref[c, :] = mm(kdd, uu, TN, P_["z"])
        return 0

    parts(0, 0)
    second.middle()
    first.middle()
    parts(1, 0)
    state = jnp.zeros((C, v_ref.shape[1]), F32)
    for i in range(nb):
        c = pl.ds(i * C, C)
        s_ref[c, :] = state
        if i < nb - 1:
            state = z_ref[c, :] + mm(f_ref[c, :], state, precision=P_["chain"])
    ring.middle()

    def last(i, _):
        cs = [pl.ds(pl.multiple_of((i * group + j) * C, C), C) for j in range(group)]
        for c in cs:
            q, k, s = q_ref[c, :], k_ref[c, :], s_ref[c, :]
            table, scale, _, _ = decay_parts(g_ref[c, :], row, col)
            u = u_ref[c, :] - mm(w_ref[c, :], s, precision=P_["ws"])
            u_ref[c, :] = u
            scores = mm(q, k, NT, P_["qk"]) * table
            o_ref[c, :] = mm(q * scale, s, precision=P_["o"]) + mm(scores, u, precision=P_["o"])
        return 0

    lax.fori_loop(0, nb // group, last, 0)
    each_block(nb, lambda i: after_delta(i, o_ref, pb_ref, gain_ref, mixed_ref))
    second.late()
    first.late()
    ring.late()
    ring.finish()
    second.finish()
    first.finish()


def bwd_kernel(P_, group, q_ref, k_ref, v_ref, b_ref, g_ref, t_ref, u_ref, s_ref, f_ref, w_ref, o_ref, dm_ref,
               pa_ref, pb_ref, tq_ref, tv_ref, dec_ref, gain_ref, terms_ref, stream_ref, da_ref, db2_ref,
               dpa_ref, dpb_ref, dtq_ref, dtv_ref, ddec_ref, dgain_ref, output_ref, owna_ref, ownb_ref,
               ds_ref, x_ref, do_ref, dq_ref, dk_ref, dv_ref, db_ref, dg_ref, cq_ref, cv_ref, here, there, out, near, ends,
               a0, a1, a2, a3, a4, b0, b1, b2, b3, b4, sc_sems, a_sems, b_sems):
    place = Place()
    greet(place, ("x", "y", "z"))
    sum_a = PlaneSum(place, "y", da_ref, (a0, a1, a2, a3, a4), owna_ref, a_sems)
    sum_b = PlaneSum(place, "x", db2_ref, (b0, b1, b2, b3, b4), ownb_ref, b_sems)
    ring = Scatter(place, terms_ref, (here, there, out, near, ends), sc_sems)
    ring.start()
    sum_a.start()
    sum_b.start()
    nb = q_ref.shape[0] // C
    for ref in (dtq_ref, dtv_ref, ddec_ref, dgain_ref):
        ref[...] = jnp.zeros_like(ref)
    each_block(nb, lambda i: after_delta_back(i, dm_ref, o_ref, pb_ref, gain_ref, do_ref, dpb_ref, dgain_ref))
    row, col = chunk_masks()

    def first(i, _):
        cs = [pl.ds(pl.multiple_of((i * group + j) * C, C), C) for j in range(group)]
        for c in cs:
            q, k, do = q_ref[c, :], k_ref[c, :], do_ref[c, :]
            table, scale, _, _ = decay_parts(g_ref[c, :], row, col)
            scores = mm(q, k, NT, P_["qk"]) * table
            x = mm(scores, do, TN, P_["bx"])
            x_ref[c, :] = x
            ds_ref[c, :] = mm(q * scale, do, TN, P_["bx"]) - mm(w_ref[c, :], x, TN, P_["bx"])
        return 0

    lax.fori_loop(0, nb // group, first, 0)
    ring.middle()
    sum_a.middle()
    sum_b.middle()
    carry = jnp.zeros((C, v_ref.shape[1]), F32)
    for i in reversed(range(nb)):
        c = pl.ds(i * C, C)
        own = ds_ref[c, :]
        ds_ref[c, :] = carry
        if i > 0:
            carry = own + mm(f_ref[c, :], carry, TN, P_["chain"])
    def last(i, _):
        cs = [pl.ds(pl.multiple_of((i * group + j) * C, C), C) for j in range(group)]
        for c in cs:
            q, k, v, b, do = q_ref[c, :], k_ref[c, :], v_ref[c, :], b_ref[c, :], do_ref[c, :]
            t, u, s, ds = t_ref[c, :], u_ref[c, :], s_ref[c, :], ds_ref[c, :]
            table, scale, tail, total = decay_parts(g_ref[c, :], row, col)
            p = P_["bl"]
            qk = mm(q, k, NT, p)
            kk = mm(k, k, NT, p)
            ks = mm(k, s, precision=p)
            qs = mm(q, s, precision=p)
            kd = k * tail
            du = x_ref[c, :] + mm(kd, ds, precision=p)
            dr = mm(t, du, TN, P_["bt"])
            dp = jnp.where(row >= col, mm(do, u, NT, p), 0.0)
            da = jnp.where(row > col, -mm(dr, u, NT, p), 0.0)
            dqk = dp * table
            dkk = da * b * table
            n = dqk * qk + dkk * kk
            dkd = mm(u, ds, NT, p)
            dq_ref[c, :] = scale * mm(do, s, NT, p) + mm(dqk, k, precision=p)
            bdr = wide(b) * dr
            dk_ref[c, :] = (
                mm(dqk, q, TN, p)
                + mm(dkk, k, precision=p)
                + mm(dkk, k, TN, p)
                + dkd * tail
                - scale * mm(bdr, s, NT, p)
            )
            dv_ref[c, :] = bdr
            sc2 = wide(scale)
            db = jnp.sum(dr * (v - sc2 * ks), 1, keepdims=True) + jnp.sum(da * table * kk, 1, keepdims=True)
            db_ref[c, :] = jnp.broadcast_to(db, (C, C))
            tails = jnp.sum(dkd * kd, 1, keepdims=True)
            dcum = (
                jnp.sum(n, 1, keepdims=True)
                - jnp.sum(n.T, 1, keepdims=True)
                + jnp.sum(sc2 * (do * qs - bdr * ks), 1, keepdims=True)
                - tails
            )
            dcum = jnp.broadcast_to(dcum, (C, C))
            extra = jnp.sum(tails) + jnp.sum(ds * s * wide(jnp.broadcast_to(total, (C, C))))
            upper = (row <= col).astype(F32)
            dg_ref[c, :] = mm(upper, dcum) + extra
        return 0

    half = nb // group // 2
    ring.late()
    lax.fori_loop(0, half, last, 0)
    sum_a.late()
    sum_b.late()
    lax.fori_loop(half, nb // group, last, 0)
    each_block(
        nb,
        lambda i: before_delta_back(
            i, pa_ref, pb_ref, tq_ref, tv_ref, dec_ref, b_ref, g_ref, dq_ref, dk_ref, dv_ref, db_ref, dg_ref,
            cq_ref, cv_ref, dpa_ref, dtq_ref, dtv_ref, ddec_ref,
        ),
    )

    def conv_step(i):
        conv_back(i, nb, cq_ref, tq_ref[...], dpa_ref)
        conv_back(i, nb, cv_ref, tv_ref[...], dpb_ref)

    each_block(nb, conv_step)
    output_ref[...] = (stream_ref[...] + ring.finish()).astype(BF)
    sum_a.finish()
    sum_b.finish()


def grads_kernel(f_ref, m_ref, g_ref, gu_ref, mixed_ref, hidden_ref, a_ref, b_ref):
    one = lambda x, y: lax.dot_general(x[...], y[...], TN, preferred_element_type=F32).astype(BF)
    a_ref[...] = one(f_ref, gu_ref)
    n = mixed_ref.shape[1]
    b_ref[:, :n] = one(m_ref, mixed_ref)
    b_ref[:, n:] = one(g_ref, hidden_ref)


def feed_forward_kernel(f_ref, g_ref, gu_ref, od_ref, hidden_ref, dgu_ref, back_ref, branch_ref):
    one = functools.partial(lax.dot_general, preferred_element_type=F32)
    half = gu_ref.shape[1] // 2
    down = od_ref[:, od_ref.shape[1] - half :]
    gate_up = one(f_ref[...], gu_ref[...], NN)
    gate, up = gate_up[:, :half], gate_up[:, half:]
    grad = one(g_ref[...], down, NN)
    s = sigmoid(gate)
    gs = gate * s
    hidden = (gs * up).astype(BF)
    hidden_ref[...] = hidden
    dgu_ref[:, :half] = (grad * up * silu_slope(gate, s)).astype(BF)
    dgu_ref[:, half:] = (grad * gs).astype(BF)
    back_ref[...] = one(dgu_ref[...], gu_ref[...], NT).astype(BF)
    branch_ref[...] = one(hidden, down, NT).astype(BF)


KEYS = ("kk", "inv", "w", "u", "f", "z", "chain", "ws", "qk", "o", "bx", "bl", "bt")
PRECS = {key: X3 for key in KEYS}
VM = pl.BlockSpec(memory_space=pltpu.VMEM)
ANY = pl.BlockSpec(memory_space=pl.ANY)


def call(kernel, name, number, ins, in_specs, outs, out_specs, scratch):
    return pl.pallas_call(
        kernel,
        name=name,
        out_shape=[jax.ShapeDtypeStruct(s, t) for s, t in outs],
        in_specs=in_specs,
        out_specs=out_specs,
        scratch_shapes=scratch,
        compiler_params=pltpu.CompilerParams(
            collective_id=number, has_side_effects=True, vmem_limit_bytes=48 * 2**20
        ),
    )(*ins)


def dot(a, b, dims=NN):
    return lax.dot_general(a, b, dims, preferred_element_type=F32)


def padded(x, width):
    return jnp.pad(x, ((0, 0), (0, width - x.shape[1])))


def up_to(n, k):
    return -(-n // k) * k


def body(
    block_input,
    mixer_gain,
    query_key_weight,
    value_gate_weight,
    beta_decay_weight,
    conv_query_key,
    conv_value,
    decay_log,
    decay_bias,
    out_gain,
    out_weight,
    forward_gain,
    gate_up_weight,
    down_weight,
    out_cotangent,
):
    d = block_input.shape[2]
    n = block_input.shape[1] * 8
    nqk, nvg, nbd = query_key_weight.shape[-1], value_gate_weight.shape[-1], beta_decay_weight.shape[-1]
    ff = gate_up_weight.shape[-1]
    dv = out_weight.shape[2]
    own_d = query_key_weight.shape[1]
    wide_a = up_to(nqk + nbd, 128)
    first_a = padded(jnp.concatenate([query_key_weight[0, :, 0], beta_decay_weight[0, :, 0]], 1), wide_a)
    first_b = value_gate_weight[0, :, 0]
    real, ff = ff, up_to(ff, 128)
    rest_a = jnp.pad(gate_up_weight[0], ((0, 0), (0, 0), (0, ff - real))).reshape(-1, 2 * ff)
    rest_b = padded(jnp.concatenate([out_weight[0, 0].T, down_weight[0].T], 1), dv + ff)
    taps = conv_query_key.shape[1]
    heads = jnp.concatenate(
        [
            conv_query_key[0, :, 0].reshape(-1, 128),
            conv_value[0, :, 0].reshape(-1, 128),
            padded(jnp.concatenate([decay_log, decay_bias], 1), 128),
        ]
    )
    head_rows = up_to(heads.shape[0], 8)
    heads = jnp.pad(heads, ((0, head_rows - heads.shape[0]), (0, 0)))
    sems = pltpu.SemaphoreType.DMA
    block = (ROWS, d)

    shard = lambda w: ((own_d, w), BF)
    plane = lambda w: ((2, 4, 2, own_d, w), BF)
    scratch = lambda w: pltpu.VMEM((own_d, w), BF)
    x, heads, w_a, w_b, rest_a, rest_b, g, rows = call(
        entry_kernel,
        "entry_exchange",
        0,
        (block_input[0], mixer_gain, heads, first_a, first_b, rest_a, rest_b, out_cotangent[0]),
        [VM, VM, VM, VM, VM, ANY, ANY, ANY],
        [(block, BF), (heads.shape, F32), plane(wide_a), plane(nvg), shard(2 * ff), shard(dv + ff), (block, BF), ((n, d), BF)],
        [VM, VM] + [ANY] * 6,
        [pltpu.VMEM(block, BF), scratch(wide_a), scratch(nvg), sems((2, 7)), RING_SEMS, RING_SEMS, GATHER_SEMS],
    )
    w_a, w_b = w_a.reshape(d, wide_a), w_b.reshape(d, nvg)
    size = taps * nqk // 128
    conv_qk, conv_v = heads[:size].reshape(taps, nqk), heads[size : 2 * size].reshape(taps, dv)

    decays = heads[2 * size : 2 * size + 1]
    pre_a, pre_b = dot(rows, w_a), dot(rows, w_b)
    f = lambda width: ((n, width), F32)
    kept = [f(C), f(C), f(dv), f(C), f(C), f(dv), f(C), f(dv), f(dv), f(C), f(C)]
    mixed, q, k, v, b, ld, delta_out, t, u, s, fm, w, g_rows, w_gu, w_od = call(
        functools.partial(fwd_kernel, PRECS, 4),
        "delta_forward",
        1,
        (pre_a, pre_b, conv_qk, conv_v, decays, out_gain, g, rest_a, rest_b),
        [VM] * 6 + [ANY] * 3,
        [((n, dv), BF)] + kept + [((n, d), BF), plane(2 * ff), plane(dv + ff)],
        [VM] * 12 + [ANY] * 3,
        [pltpu.VMEM((n, dv), F32), RING_SEMS, RING_SEMS, GATHER_SEMS],
    )
    w_gu, w_od = w_gu.reshape(d, 2 * ff), w_od.reshape(d, dv + ff)
    w_out = w_od[:, :dv]
    stream, forward_rows = call(
        sum_norm_gather_kernel,
        "sum_norm_gather",
        2,
        (dot(mixed, w_out, NT).astype(BF), x, forward_gain),
        [ANY, VM, VM],
        [(block, F32), ((n, d), BF)],
        [VM, ANY],
        [pltpu.VMEM(block, BF)] + scatter_scratch(d) + [SCATTER_SEMS, GATHER_SEMS],
    )
    tile = n // 4
    row_tile = lambda width: pl.BlockSpec((tile, width), lambda i: (i, 0))
    fixed = lambda rows, width: pl.BlockSpec((rows, width), lambda i: (0, 0))
    hidden, grad_gu, grad_terms, branch_terms = pl.pallas_call(
        feed_forward_kernel,
        name="feed_forward",
        grid=(4,),
        out_shape=[jax.ShapeDtypeStruct((n, width), BF) for width in (ff, 2 * ff, d, d)],
        in_specs=[row_tile(d), row_tile(d), fixed(d, 2 * ff), fixed(d, dv + ff)],
        out_specs=[row_tile(width) for width in (ff, 2 * ff, d, d)],
        compiler_params=pltpu.CompilerParams(vmem_limit_bytes=40 * 2**20),
    )(forward_rows, g_rows, w_gu, w_od)
    grad_stream, grad_fgain, m_rows = call(
        sum_back_gather_kernel,
        "sum_back_gather",
        3,
        (grad_terms, stream, forward_gain, g),
        [ANY, VM, VM, VM],
        [(block, F32), ((1, d), F32), ((n, d), BF)],
        [VM, VM, ANY],
        [pltpu.VMEM(block, BF)] + scatter_scratch(d) + [SCATTER_SEMS, GATHER_SEMS],
    )
    wide = d // 4
    column = pl.BlockSpec((n, wide), lambda i: (0, i))
    whole = lambda width: pl.BlockSpec((n, width), lambda i: (0, 0))
    grads_a, grads_b = pl.pallas_call(
        grads_kernel,
        name="rest_gradients",
        grid=(4,),
        out_shape=[jax.ShapeDtypeStruct((d, 2 * ff), BF), jax.ShapeDtypeStruct((d, dv + ff), BF)],
        in_specs=[column, column, column, whole(2 * ff), whole(dv), whole(ff)],
        out_specs=[pl.BlockSpec((wide, 2 * ff), lambda i: (i, 0)), pl.BlockSpec((wide, dv + ff), lambda i: (i, 0))],
        compiler_params=pltpu.CompilerParams(vmem_limit_bytes=40 * 2**20),
    )(forward_rows, m_rows, g_rows, grad_gu, mixed, hidden)
    grads_a = grads_a.reshape(2, 4, 2, own_d, 2 * ff)
    grads_b = grads_b.reshape(2, 4, 2, own_d, dv + ff)
    d_a, d_b, grad_cqk, grad_cv, grad_decays, grad_ogain, output, own_a, own_b = call(
        functools.partial(bwd_kernel, PRECS, 4),
        "delta_backward",
        4,
        (q, k, v, b, ld, t, u, s, fm, w, delta_out, dot(m_rows, w_out), pre_a, pre_b, conv_qk, conv_v, decays, out_gain,
         branch_terms, stream, grads_a, grads_b),
        [VM] * 18 + [ANY, VM, VM, VM],
        [((n, wide_a), BF), ((n, nvg), BF), (conv_qk.shape, F32), (conv_v.shape, F32), ((1, 128), F32), ((1, dv), F32),
         (block, BF), shard(2 * ff), shard(dv + ff)],
        [VM] * 9,
        [pltpu.VMEM((n, width), F32) for width in (dv, dv, dv, C, C, dv, C, C, 2 * C, dv)]
        + scatter_scratch(d)
        + plane_scratch("y", own_d, 2 * ff) + plane_scratch("x", own_d, dv + ff)
        + [SCATTER_SEMS, RING_SEMS, RING_SEMS],
    )
    gain_rows = up_to((2 * d + dv) // 128, 8)
    zero = jnp.zeros((1, 128), F32)
    small = jnp.concatenate(
        [
            jnp.zeros((d // 128, 128), F32),
            grad_fgain.reshape(-1, 128),
            grad_ogain.reshape(-1, 128),
            jnp.zeros((gain_rows - (2 * d + dv) // 128, 128), F32),
            grad_cqk.reshape(-1, 128),
            grad_cv.reshape(-1, 128),
            grad_decays,
            jnp.zeros((head_rows - 2 * size - 1, 128), F32),
        ]
    )
    small_rows = small.shape[0]
    final, input_grad, in_a, in_b, rest_a, rest_b, sums = call(
        exit_kernel,
        "exit_exchange",
        5,
        (
            (dot(d_a, w_a, NT) + dot(d_b, w_b, NT)).astype(BF),
            x,
            mixer_gain,
            grad_stream,
            output,
            dot(rows, d_a, TN).astype(BF).reshape(2, 4, 2, own_d, wide_a),
            dot(rows, d_b, TN).astype(BF).reshape(2, 4, 2, own_d, nvg),
            own_a,
            own_b,
            small,
        ),
        [ANY, VM, VM, VM, VM, VM, VM, VM, VM, VM],
        [(block, BF), (block, BF), shard(wide_a), shard(nvg), shard(2 * ff), shard(dv + ff), ((small_rows, 128), F32)],
        [ANY] * 6 + [VM],
        [pltpu.VMEM(block, BF)]
        + scatter_scratch(d)
        + plane_scratch("y", own_d, wide_a) + plane_scratch("x", own_d, nvg)
        + [scratch(wide_a), scratch(nvg)]
        + [
            pltpu.VMEM((small_rows, 128), F32),
            pltpu.VMEM((16, small_rows, 128), F32),
            pltpu.VMEM((small_rows, 128), F32),
            pltpu.VMEM((7, gain_rows, 128), F32),
            SCATTER_SEMS,
            sems((2, 6)),
            RING_SEMS,
            RING_SEMS,
            PLANE_SEMS,
            sems((2, 7)),
        ],
    )
    in_a, in_b, rest_a, rest_b = (a.astype(F32) for a in (in_a, in_b, rest_a, rest_b))
    k8 = d // 128
    hs = sums[gain_rows:]
    return (
        final.astype(F32)[None],
        input_grad.astype(F32)[None],
        sums[:k8].reshape(1, d),
        in_a[None, :, None, :nqk],
        in_b[None, :, None],
        in_a[None, :, None, nqk : nqk + nbd],
        hs[:size].reshape(1, taps, 1, nqk),
        hs[size : 2 * size].reshape(1, taps, 1, dv),
        hs[2 * size : 2 * size + 1, :1],
        hs[2 * size : 2 * size + 1, 1:2],
        sums[2 * k8 : 2 * k8 + dv // 128].reshape(1, dv),
        rest_b[:, :dv].T[None, None],
        sums[k8 : 2 * k8].reshape(1, d),
        rest_a.reshape(1, -1, 2, ff)[..., :real],
        rest_b[:, dv : dv + real].T[None],
    )


def solution(mesh):
    parts = Mesh(mesh.devices.reshape(2, 4, 2, 2, 4), AXES)
    dp, tp = ("ylo", "x", "core"), ("yhi", "z")
    stream = P(dp, tp, None)
    head = P(None, tp)
    proj = P(None, dp, tp, None)
    conv = P(None, None, tp, None)
    out_w, gu_w, down_w = P(None, tp, None, dp), P(None, dp, None, tp), P(None, tp, dp)
    return jax.shard_map(
        body,
        mesh=parts,
        in_specs=(stream, P(), proj, proj, proj, conv, conv, head, head, P(), out_w, P(), gu_w, down_w, stream),
        out_specs=(stream, stream, P(), proj, proj, proj, conv, conv, head, head, P(), out_w, P(), gu_w, down_w),
        check_vma=False,
    )
```
